32 devices in a mesh: section: 4 (over y, core), block: 8 (over z, x).
Axes of the slice: x: 2, y: 2, z: 4, core: 2. Of those that a mesh axis runs over, the one named last changes fastest.
Arguments:
- inputs: bfloat16 [4, 16384, 128], P('section', 'block'), may hold values from -6 to 6
- cotangent: bfloat16 [4, 16384, 128], P('section', 'block'), may hold values from -6 to 6
- right_factor: bfloat16 [2, 4, 128, 128, 128], P(None, 'section', 'block'), may hold values from -0.5 to 0.5
- left_factor: bfloat16 [2, 4, 128, 128, 128], P(None, 'section', 'block'), may hold values from -0.5 to 0.5
Outputs:
- outputs: bfloat16 [4, 16384, 128], P('section', 'block')
- input_grad: bfloat16 [4, 16384, 128], P('section', 'block')
- right_grad: float32 [2, 4, 128, 128, 128], P(None, 'section', 'block')
- left_grad: float32 [2, 4, 128, 128, 128], P(None, 'section', 'block')
The draws below stay inside these ranges and needn't reach their ends.
All inputs are finite; a program needn't handle non-finite values.
Results may differ from the reference program's by a relative error of at most 0.04.
Values may be sent and summed in bfloat16 or wider, within the bound.
No kernel may reach another device: no remote copies, remote signals or barrier semaphores. Data moves between devices by JAX's collectives and lax.ppermute only.
A program may use at most 64 MiB of HBM per device.

```python
import jax
import jax.numpy as jnp

D = 16384
BS = 128
NB = 128
MB = 128
LOOPS = 2
MICRO = 4
LAYERS = 8
N_SECTION = 4


def levels(key, shape, pieces, low, largest):
    gain = 1.0
    for position, blocks in pieces:
        steps = jax.random.uniform(jax.random.fold_in(jax.random.fold_in(key, 6), position), (blocks,), jnp.float32, low / len(pieces), largest / len(pieces))
        gain = gain * jnp.repeat(jnp.exp(steps), shape[position] // blocks).reshape((-1,) + (1,) * (len(shape) - 1 - position))
    return gain


def gaussian(rng, shape, deviation, most, pieces=(), held_as=jnp.bfloat16):
    gain = levels(rng, shape, pieces, -0.22, 0.18) if pieces else 1.0
    values = jax.random.normal(rng, shape, jnp.float32) * deviation * gain
    return jnp.minimum(jnp.maximum(values, -most), most).astype(held_as)


def setup_inputs(seed: int = 0) -> dict:
    streams_of = jax.random.split(jax.random.key(seed), 5)
    return {
        "inputs": gaussian(streams_of[0], (MICRO, D, MB), 1.0, 6.0, ((0, 4), (1, 8))),
        "cotangent": gaussian(streams_of[1], (MICRO, D, MB), 1.0, 6.0, ((0, 4), (1, 8))),
        "right_factor": gaussian(streams_of[2], (LOOPS, N_SECTION, NB, BS, BS), BS ** -0.5, 0.5, ((1, 4), (2, 8))),
        "left_factor": gaussian(streams_of[3], (LOOPS, N_SECTION, BS, NB, NB), NB ** -0.5, 0.5, ((1, 4), (2, 8))),
    }


def layer_forward(layer_input, right_block, left_block):
    acts = layer_input.reshape(NB, BS, -1).astype(jnp.float32)
    mixed = jnp.einsum('bjk,bjr->bkr', right_block.astype(jnp.float32), acts).astype(jnp.bfloat16)
    activated = jax.nn.silu(mixed.astype(jnp.float32)).astype(jnp.bfloat16)
    second = jnp.einsum('kbc,bkr->ckr', left_block.astype(jnp.float32), activated.astype(jnp.float32)).astype(jnp.bfloat16)
    result = (acts + second.astype(jnp.float32)).astype(jnp.bfloat16)
    return result.reshape(D, -1)


def layer_backward(layer_input, grad_out, right_block, left_block):
    acts = layer_input.reshape(NB, BS, -1).astype(jnp.float32)
    right_wide = right_block.astype(jnp.float32)
    left_wide = left_block.astype(jnp.float32)
    mixed = jnp.einsum('bjk,bjr->bkr', right_wide, acts).astype(jnp.bfloat16).astype(jnp.float32)
    activated = jax.nn.silu(mixed).astype(jnp.bfloat16).astype(jnp.float32)
    grad_wide = grad_out.reshape(NB, BS, -1).astype(jnp.float32)
    left_term = jnp.einsum('bkr,ckr->kbc', activated, grad_wide)
    grad_act = jnp.einsum('kbc,ckr->bkr', left_wide, grad_wide)
    sigmoid = jax.nn.sigmoid(mixed)
    grad_mixed = (grad_act * sigmoid * (1.0 + mixed * (1.0 - sigmoid))).astype(jnp.bfloat16).astype(jnp.float32)
    right_term = jnp.einsum('bjr,bkr->bjk', acts, grad_mixed)
    grad_in = (grad_wide + jnp.einsum('bjk,bkr->bjr', right_wide, grad_mixed)).astype(jnp.bfloat16)
    return grad_in.reshape(D, -1), right_term, left_term


def reference(inputs, cotangent, right_factor, left_factor):
    right_grad = jnp.zeros(right_factor.shape, jnp.float32)
    left_grad = jnp.zeros(left_factor.shape, jnp.float32)
    results = []
    grads_in = []
    for batch_slot in range(MICRO):
        current = inputs[batch_slot]
        stored = []
        for layer_index in range(LAYERS):
            loop_index = layer_index // N_SECTION
            section_index = layer_index % N_SECTION
            stored.append(current)
            current = layer_forward(current, right_factor[loop_index, section_index], left_factor[loop_index, section_index])
        results.append(current)
        grad_now = cotangent[batch_slot]
        for layer_index in range(LAYERS - 1, -1, -1):
            loop_index = layer_index // N_SECTION
            section_index = layer_index % N_SECTION
            grad_now, right_term, left_term = layer_backward(stored[layer_index], grad_now, right_factor[loop_index, section_index], left_factor[loop_index, section_index])
            right_grad = right_grad.at[loop_index, section_index].add(right_term)
            left_grad = left_grad.at[loop_index, section_index].add(left_term)
        grads_in.append(grad_now)
    return jnp.stack(results), jnp.stack(grads_in), right_grad, left_grad
```

```python
import jax
import jax.numpy as jnp
from jax import lax
from jax.sharding import Mesh, PartitionSpec as P

F32 = jnp.float32
BF16 = jnp.bfloat16
PLANE = ("s", "x")


def swap(chunks, axes):
    return lax.all_to_all(chunks, axes, split_axis=0, concat_axis=0, tiled=True)


def silu_slope(values):
    sigmoid = jax.nn.sigmoid(values)
    return sigmoid * (1.0 + values * (1.0 - sigmoid))


def plane_order(size, sections, peers):
    sub = size // (sections * sections * peers)
    natural = jnp.arange(size).reshape(sections, peers, sections, sub)
    order = natural.transpose(2, 1, 0, 3).reshape(size)
    return (order[:, None] == jnp.arange(size)[None, :]).astype(BF16)


def to_columns(values):
    own, full, rows = values.shape
    moved = swap(values.transpose(1, 0, 2), PLANE)
    return moved.reshape(full // own, own, own, rows).transpose(1, 0, 2, 3).reshape(own, full, rows)


def body(inputs, cotangent, right_factor, left_factor):
    sections = lax.axis_size("s")
    peers = lax.axis_size("x")
    loops, _, own, size, _ = right_factor.shape
    rows = inputs.shape[2]
    sub = own // sections
    layers = loops * sections
    order = plane_order(size, sections, peers)

    def permuted(blocks):
        return jnp.einsum("aj,bjr->bar", order, blocks, preferred_element_type=F32).astype(BF16)

    def natural(blocks, kind):
        return jnp.einsum("aj,bar->bjr", order, blocks, preferred_element_type=F32).astype(kind)

    def enter(acts):
        parts = permuted(acts.reshape(own, size, rows)).reshape(sections, sub, size, rows)
        return swap(swap(parts, "s"), "t").reshape(own, size, rows)

    def leave(acts):
        parts = swap(swap(acts.reshape(sections, sub, size, rows), "t"), "s")
        return natural(parts.reshape(own, size, rows), BF16).reshape(1, own * size, rows)

    both = jnp.stack([right_factor[:, 0], left_factor[:, 0]], axis=1)
    both = jnp.einsum("aj,lfbjk,ck->lfbac", order, both, order, preferred_element_type=F32).astype(BF16)
    both = both.reshape(loops, 2, sections, sub, size, size).transpose(0, 2, 1, 3, 4, 5)
    weights = []
    for loop in range(loops):
        moved = swap(both[loop], "s")
        for section in range(sections):
            full = lax.all_gather(moved[section], "t", axis=0, tiled=False)
            weights.append((full[:, 0].reshape(own, size, size), full[:, 1].reshape(own, size, size)))

    current = enter(inputs)
    grad = enter(cotangent)
    stored = []
    for right, left in weights:
        mixed = jnp.einsum("bjk,bjr->bkr", right, current, preferred_element_type=F32).astype(BF16)
        columns = to_columns(mixed)
        stored.append((current, columns))
        activated = jax.nn.silu(columns.astype(F32)).astype(BF16)
        second = jnp.einsum("kbc,kbr->kcr", left, activated, preferred_element_type=F32).astype(BF16)
        returned = to_columns(second)
        current = (current.astype(F32) + returned.astype(F32)).astype(BF16)
    outputs = leave(current)

    sums = [None] * layers
    for layer in reversed(range(layers)):
        right, left = weights[layer]
        acts, columns = stored[layer]
        grad_columns = to_columns(grad)
        wide = columns.astype(F32)
        activated = jax.nn.silu(wide).astype(BF16)
        left_term = jnp.einsum("kbr,kcr->kbc", activated, grad_columns, preferred_element_type=F32)
        grad_act = jnp.einsum("kbc,kcr->kbr", left, grad_columns, preferred_element_type=F32)
        grad_mixed = to_columns((grad_act * silu_slope(wide)).astype(BF16))
        right_term = jnp.einsum("bjr,bkr->bjk", acts, grad_mixed, preferred_element_type=F32)
        branch = jnp.einsum("bjk,bkr->bjr", right, grad_mixed, preferred_element_type=F32)
        grad = (grad.astype(F32) + branch).astype(BF16)
        terms = jnp.stack(
            [
                right_term.astype(BF16).reshape(sections, sub, size, size),
                left_term.astype(BF16).reshape(sections, sub, size, size),
            ],
            axis=1,
        )
        sums[layer] = lax.psum_scatter(terms, "t", scatter_dimension=0, tiled=False)
    input_grad = leave(grad)

    halves = []
    for loop in range(loops):
        moved = swap(jnp.stack(sums[loop * sections : (loop + 1) * sections]), "s")
        blocks = moved.transpose(1, 0, 2, 3, 4).reshape(2, own, size, size)
        halves.append(
            jnp.einsum("aj,fbac,ck->fbjk", order, blocks, order, preferred_element_type=F32)
        )
    grads = jnp.stack(halves)
    return (outputs, input_grad, grads[:, 0][:, None], grads[:, 1][:, None])


def solution(mesh):
    sections = mesh.shape["section"]
    peers = mesh.shape["block"] // sections
    planes = Mesh(mesh.devices.reshape(sections, sections, peers), ("s", "t", "x"))
    acts = P("s", ("t", "x"), None)
    factor = P(None, "s", ("t", "x"), None, None)
    return jax.shard_map(
        body,
        mesh=planes,
        in_specs=(acts, acts, factor, factor),
        out_specs=(acts, acts, factor, factor),
        check_vma=False,
    )
```

```python
import jax
import jax.numpy as jnp
from jax import lax
from jax.sharding import Mesh, PartitionSpec as P

F32 = jnp.float32
BF16 = jnp.bfloat16
PLANE = ("s", "x")
MOST_PAIRWISE = 8


def pairwise(value, axes, count, mask):
    return lax.ppermute(value, axes, [(i, i ^ mask) for i in range(count)])


def silu_slope(values):
    sigmoid = jax.nn.sigmoid(values)
    return sigmoid * (1.0 + values * (1.0 - sigmoid))


def plane_orders(size, sections, peers):
    sub = size // (sections * sections * peers)
    count = sections * peers
    natural = jnp.arange(size).reshape(sections, peers, sections, sub)
    by_peer = natural.transpose(2, 1, 0, 3).reshape(count, size // count)
    me = jnp.arange(sections)[:, None] * peers + lax.axis_index("x")
    if count > MOST_PAIRWISE:
        me = jnp.zeros_like(me)
    order = by_peer[me ^ jnp.arange(count)[None, :]].reshape(sections, size)
    return (order[:, :, None] == jnp.arange(size)[None, None, :]).astype(BF16)


def exchange(values):
    own, full, rows = values.shape
    count = full // own
    pieces = values.transpose(1, 0, 2).reshape(count, own, own, rows)
    if count > MOST_PAIRWISE:
        moved = lax.all_to_all(pieces, PLANE, split_axis=0, concat_axis=0, tiled=True)
        return moved.transpose(1, 0, 2, 3).reshape(own, full, rows)
    moved = [pieces[0]] + [pairwise(pieces[m], PLANE, count, m) for m in range(1, count)]
    return jnp.concatenate(moved, axis=1)


def body(inputs, cotangent, right_factor, left_factor):
    sections = lax.axis_size("s")
    peers = lax.axis_size("x")
    loops, _, own, size, _ = right_factor.shape
    rows = inputs.shape[2]
    sub = own // sections
    layers = loops * sections
    s_index = lax.axis_index("s")
    t_index = lax.axis_index("t")
    orders = plane_orders(size, sections, peers)
    my_order = lax.dynamic_index_in_dim(orders, s_index, 0, keepdims=False)

    def turned(parts, send_by, place_by, target):
        moved = []
        for mask in range(sections):
            value = lax.dynamic_index_in_dim(parts, send_by ^ mask, 0, keepdims=False)
            pairs = [
                (s * sections + t, target(s, t, mask)) for s in range(sections) for t in range(sections)
            ]
            moved.append(lax.ppermute(value, ("s", "t"), pairs))
        moved = jnp.stack(moved)
        return jnp.stack(
            [
                lax.dynamic_index_in_dim(moved, place_by ^ part, 0, keepdims=False)
                for part in range(sections)
            ]
        )

    def enter(acts):
        parts = acts.reshape(sections, sub, size, rows)
        parts = turned(parts, t_index, s_index, lambda s, t, mask: (t ^ mask) * sections + s)
        parts = parts.reshape(own, size, rows)
        return jnp.einsum("aj,bjr->bar", my_order, parts, preferred_element_type=F32).astype(BF16)

    def leave(acts):
        acts = jnp.einsum("aj,bar->bjr", my_order, acts, preferred_element_type=F32).astype(BF16)
        parts = acts.reshape(sections, sub, size, rows)
        parts = turned(parts, s_index, t_index, lambda s, t, mask: t * sections + (s ^ mask))
        return parts.reshape(1, own * size, rows)

    both = jnp.stack([right_factor[:, 0], left_factor[:, 0]], axis=1)
    both = both.reshape(loops, 2, sections, sub, size, size)
    both = jnp.einsum("saj,lfsbjk,sck->lsfbac", orders, both, orders, preferred_element_type=F32)
    both = both.astype(BF16)
    weights = []
    for loop in range(loops):
        moved = lax.all_to_all(both[loop], "s", split_axis=0, concat_axis=0, tiled=True)
        for section in range(sections):
            full = lax.all_gather(moved[section], "t", axis=0, tiled=False)
            weights.append((full[:, 0].reshape(own, size, size), full[:, 1].reshape(own, size, size)))

    current = enter(inputs)
    grad = enter(cotangent)
    stored = []
    for right, left in weights:
        mixed = jnp.einsum("bjk,bjr->bkr", right, current, preferred_element_type=F32).astype(BF16)
        columns = exchange(mixed)
        stored.append((current, columns))
        activated = jax.nn.silu(columns.astype(F32)).astype(BF16)
        second = jnp.einsum("kbc,kbr->kcr", left, activated, preferred_element_type=F32).astype(BF16)
        returned = exchange(second)
        current = (current.astype(F32) + returned.astype(F32)).astype(BF16)
    outputs = leave(current)

    def reduced(terms):
        step = 1
        parts = terms
        while step < sections:
            pairs = parts.reshape((parts.shape[0] // 2, 2) + parts.shape[1:])
            bit = (t_index // step) % 2
            keep = lax.dynamic_index_in_dim(pairs, bit, 1, keepdims=False)
            give = lax.dynamic_index_in_dim(pairs, 1 - bit, 1, keepdims=False)
            got = pairwise(give, "t", sections, step)
            parts = (keep.astype(F32) + got.astype(F32)).astype(BF16)
            step *= 2
        return parts[0]

    sums = [None] * layers
    for layer in reversed(range(layers)):
        right, left = weights[layer]
        acts, columns = stored[layer]
        grad_columns = exchange(grad)
        wide = columns.astype(F32)
        activated = jax.nn.silu(wide).astype(BF16)
        left_term = jnp.einsum("kbr,kcr->kbc", activated, grad_columns, preferred_element_type=F32)
        grad_act = jnp.einsum("kbc,kcr->kbr", left, grad_columns, preferred_element_type=F32)
        grad_mixed = exchange((grad_act * silu_slope(wide)).astype(BF16))
        right_term = jnp.einsum("bjr,bkr->bjk", acts, grad_mixed, preferred_element_type=F32)
        branch = jnp.einsum("bjk,bkr->bjr", right, grad_mixed, preferred_element_type=F32)
        grad = (grad.astype(F32) + branch).astype(BF16)
        terms = jnp.stack(
            [
                right_term.astype(BF16).reshape(sections, sub, size, size),
                left_term.astype(BF16).reshape(sections, sub, size, size),
            ],
            axis=1,
        )
        sums[layer] = reduced(terms)
    input_grad = leave(grad)

    halves = []
    for loop in range(loops):
        mine = jnp.stack(sums[loop * sections : (loop + 1) * sections])
        moved = lax.all_to_all(mine, "s", split_axis=0, concat_axis=0, tiled=True)
        halves.append(
            jnp.einsum("saj,sfbac,sck->fsbjk", orders, moved, orders, preferred_element_type=F32)
        )
    grads = jnp.stack(halves).reshape(loops, 2, 1, own, size, size)
    return (outputs, input_grad, grads[:, 0], grads[:, 1])


def solution(mesh):
    sections = mesh.shape["section"]
    peers = mesh.shape["block"] // sections
    planes = Mesh(mesh.devices.reshape(sections, sections, peers), ("s", "t", "x"))
    acts = P("s", ("t", "x"), None)
    factor = P(None, "s", ("t", "x"), None, None)
    return jax.shard_map(
        body,
        mesh=planes,
        in_specs=(acts, acts, factor, factor),
        out_specs=(acts, acts, factor, factor),
        check_vma=False,
    )
```

```python
import jax
import jax.numpy as jnp
from jax import lax
from jax.sharding import Mesh, PartitionSpec as P

F32 = jnp.float32
BF16 = jnp.bfloat16
WIDE = ("s", "x")
GROUPS = 2
CHAINS = 1


def silu_slope(values):
    sigmoid = jax.nn.sigmoid(values)
    return sigmoid * (1.0 + values * (1.0 - sigmoid))


def group_order(size, sections, groups, peers):
    natural = jnp.arange(size).reshape(groups, peers, sections, -1)
    order = natural.transpose(2, 1, 0, 3).reshape(size)
    return (order[:, None] == jnp.arange(size)[None, :]).astype(BF16)


def exchange(values):
    own, full, rows = values.shape
    pieces = values.transpose(1, 0, 2).reshape(full // own, own, own, rows)
    moved = lax.all_to_all(pieces, WIDE, split_axis=0, concat_axis=0, tiled=True)
    return moved.transpose(1, 0, 2, 3).reshape(own, full, rows)


def body(inputs, cotangent, right_factor, left_factor):
    sections = lax.axis_size("s")
    groups = lax.axis_size("t")
    peers = lax.axis_size("x")
    loops, _, held, size, _ = right_factor.shape
    rows = inputs.shape[2]
    sub = held // sections
    own = sub * groups
    layers = loops * sections
    micros = sections // groups
    s_index = lax.axis_index("s")
    t_index = lax.axis_index("t")
    line = (s_index % micros) * groups + t_index
    order = group_order(size, sections, groups, peers)

    def turned(parts, send_by, place_by, target):
        moved = []
        for mask in range(sections):
            value = lax.dynamic_index_in_dim(parts, send_by ^ mask, 0, keepdims=False)
            pairs = [(s * groups + t, target(s, t, mask)) for s in range(sections) for t in range(groups)]
            moved.append(lax.ppermute(value, ("s", "t"), pairs))
        moved = jnp.stack(moved)
        return jnp.stack(
            [
                lax.dynamic_index_in_dim(moved, place_by ^ part, 0, keepdims=False)
                for part in range(sections)
            ]
        )

    def into(s, t, mask):
        return (((s % micros) * groups + t) ^ mask) * groups + s // micros

    def outof(s, t, mask):
        line_to = s ^ mask
        return (t * micros + line_to // groups) * groups + line_to % groups

    def enter(acts):
        parts = turned(acts.reshape(sections, sub, size, rows), line, s_index, into)
        parts = parts.reshape(micros, own, size, rows).transpose(1, 2, 0, 3)
        parts = parts.reshape(own, size, micros * rows)
        return jnp.einsum("aj,bjr->bar", order, parts, preferred_element_type=F32).astype(BF16)

    def leave(acts):
        acts = jnp.einsum("aj,bar->bjr", order, acts, preferred_element_type=F32).astype(BF16)
        parts = acts.reshape(own, size, micros, rows).transpose(2, 0, 1, 3)
        parts = turned(parts.reshape(sections, sub, size, rows), s_index, line, outof)
        return parts.reshape(1, held * size, rows)

    def split(acts):
        return jnp.split(acts, CHAINS, axis=2)

    def merge(chains):
        return jnp.concatenate(chains, axis=2)

    both = jnp.stack([right_factor[:, 0], left_factor[:, 0]], axis=1)
    both = jnp.einsum("aj,lfbjk,ck->lfbac", order, both, order, preferred_element_type=F32).astype(BF16)
    both = both.reshape(loops, 2, sections, sub, size, size).transpose(0, 2, 1, 3, 4, 5)
    weights = []
    for loop in range(loops):
        moved = [lax.dynamic_index_in_dim(both[loop], s_index, 0, keepdims=False)]
        for mask in range(1, sections):
            value = lax.dynamic_index_in_dim(both[loop], s_index ^ mask, 0, keepdims=False)
            moved.append(lax.ppermute(value, "s", [(s, s ^ mask) for s in range(sections)]))
        moved = jnp.stack(moved)
        for section in range(sections):
            part = lax.dynamic_index_in_dim(moved, s_index ^ section, 0, keepdims=False)
            full = lax.all_gather(part, "t", axis=0, tiled=False)
            weights.append((full[:, 0].reshape(own, size, size), full[:, 1].reshape(own, size, size)))

    current = split(enter(inputs))
    grad = split(enter(cotangent))
    stored = []
    for right, left in weights:
        columns = []
        following = []
        for acts in current:
            mixed = jnp.einsum("bjk,bjr->bkr", right, acts, preferred_element_type=F32).astype(BF16)
            columns.append(exchange(mixed))
        for acts, column in zip(current, columns):
            activated = jax.nn.silu(column.astype(F32)).astype(BF16)
            second = jnp.einsum("kbc,kbr->kcr", left, activated, preferred_element_type=F32).astype(BF16)
            following.append((acts.astype(F32) + exchange(second).astype(F32)).astype(BF16))
        stored.append((current, columns))
        current = following
    outputs = leave(merge(current))

    sums = [None] * layers
    for layer in reversed(range(layers)):
        right, left = weights[layer]
        right_term = 0.0
        left_term = 0.0
        following = []
        for acts, column, grad_out in zip(*stored[layer], grad):
            grad_columns = exchange(grad_out)
            wide = column.astype(F32)
            activated = jax.nn.silu(wide).astype(BF16)
            left_term += jnp.einsum("kbr,kcr->kbc", activated, grad_columns, preferred_element_type=F32)
            grad_act = jnp.einsum("kbc,kcr->kbr", left, grad_columns, preferred_element_type=F32)
            grad_mixed = exchange((grad_act * silu_slope(wide)).astype(BF16))
            right_term += jnp.einsum("bjr,bkr->bjk", acts, grad_mixed, preferred_element_type=F32)
            branch = jnp.einsum("bjk,bkr->bjr", right, grad_mixed, preferred_element_type=F32)
            following.append((grad_out.astype(F32) + branch).astype(BF16))
        grad = following
        terms = jnp.stack(
            [
                right_term.astype(BF16).reshape(groups, sub, size, size),
                left_term.astype(BF16).reshape(groups, sub, size, size),
            ],
            axis=1,
        )
        terms = terms.reshape(2 * own, size, size)
        terms = lax.psum_scatter(terms, "t", scatter_dimension=0, tiled=True)
        sums[layer] = terms.reshape(2, sub, size, size)
    input_grad = leave(merge(grad))

    halves = []
    for loop in range(loops):
        mine = jnp.stack(sums[loop * sections : (loop + 1) * sections])
        moved = lax.all_to_all(mine, "s", split_axis=0, concat_axis=0, tiled=True)
        halves.append(jnp.einsum("aj,sfbac,ck->fsbjk", order, moved, order, preferred_element_type=F32))
    grads = jnp.stack(halves).reshape(loops, 2, 1, held, size, size)
    return (outputs, input_grad, grads[:, 0], grads[:, 1])


def solution(mesh):
    sections = mesh.shape["section"]
    peers = mesh.shape["block"] // GROUPS
    grouped = Mesh(mesh.devices.reshape(sections, GROUPS, peers), ("s", "t", "x"))
    acts = P("s", ("t", "x"), None)
    factor = P(None, "s", ("t", "x"), None, None)
    return jax.shard_map(
        body,
        mesh=grouped,
        in_specs=(acts, acts, factor, factor),
        out_specs=(acts, acts, factor, factor),
        check_vma=False,
    )
```

```python
import jax
import jax.numpy as jnp
from jax import lax
from jax.sharding import Mesh, PartitionSpec as P

F32 = jnp.float32
BF16 = jnp.bfloat16
WIDE = ("s", "x")
GROUPS = 2
CHAINS = 1
LAG = 3


def silu_slope(values):
    sigmoid = jax.nn.sigmoid(values)
    return sigmoid * (1.0 + values * (1.0 - sigmoid))


def group_order(size, sections, groups, peers):
    natural = jnp.arange(size).reshape(groups, peers, sections, -1)
    order = natural.transpose(2, 1, 0, 3).reshape(size)
    return (order[:, None] == jnp.arange(size)[None, :]).astype(BF16)


def exchange(values):
    own, full, rows = values.shape
    pieces = values.transpose(1, 0, 2).reshape(full // own, own, own, rows)
    moved = lax.all_to_all(pieces, WIDE, split_axis=0, concat_axis=0, tiled=True)
    return moved.transpose(1, 0, 2, 3).reshape(own, full, rows)


def body(inputs, cotangent, right_factor, left_factor):
    sections = lax.axis_size("s")
    groups = lax.axis_size("t")
    peers = lax.axis_size("x")
    loops, _, held, size, _ = right_factor.shape
    rows = inputs.shape[2]
    sub = held // sections
    own = sub * groups
    layers = loops * sections
    micros = sections // groups
    s_index = lax.axis_index("s")
    t_index = lax.axis_index("t")
    line = (s_index % micros) * groups + t_index
    order = group_order(size, sections, groups, peers)

    def turned(parts, send_by, place_by, target):
        moved = []
        for mask in range(sections):
            value = lax.dynamic_index_in_dim(parts, send_by ^ mask, 0, keepdims=False)
            pairs = [(s * groups + t, target(s, t, mask)) for s in range(sections) for t in range(groups)]
            moved.append(lax.ppermute(value, ("s", "t"), pairs))
        moved = jnp.stack(moved)
        return jnp.stack(
            [
                lax.dynamic_index_in_dim(moved, place_by ^ part, 0, keepdims=False)
                for part in range(sections)
            ]
        )

    def into(s, t, mask):
        return (((s % micros) * groups + t) ^ mask) * groups + s // micros

    def outof(s, t, mask):
        line_to = s ^ mask
        return (t * micros + line_to // groups) * groups + line_to % groups

    def enter(acts):
        parts = turned(acts.reshape(sections, sub, size, rows), line, s_index, into)
        parts = parts.reshape(micros, own, size, rows).transpose(1, 2, 0, 3)
        parts = parts.reshape(own, size, micros * rows)
        return jnp.einsum("aj,bjr->bar", order, parts, preferred_element_type=F32).astype(BF16)

    def leave(acts):
        acts = jnp.einsum("aj,bar->bjr", order, acts, preferred_element_type=F32).astype(BF16)
        parts = acts.reshape(own, size, micros, rows).transpose(2, 0, 1, 3)
        parts = turned(parts.reshape(sections, sub, size, rows), s_index, line, outof)
        return parts.reshape(1, held * size, rows)

    def split(acts):
        return jnp.split(acts, CHAINS, axis=2)

    def merge(chains):
        return jnp.concatenate(chains, axis=2)

    def scattered(parts):
        moved = [lax.dynamic_index_in_dim(parts, s_index, 0, keepdims=False)]
        for mask in range(1, sections):
            value = lax.dynamic_index_in_dim(parts, s_index ^ mask, 0, keepdims=False)
            moved.append(lax.ppermute(value, "s", [(s, s ^ mask) for s in range(sections)]))
        moved = jnp.stack(moved)
        return [
            lax.dynamic_index_in_dim(moved, s_index ^ section, 0, keepdims=False) for section in range(sections)
        ]

    def gathered(part):
        moved = [part]
        step = 1
        while step < groups:
            other = [lax.ppermute(one, "t", [(t, t ^ step) for t in range(groups)]) for one in moved]
            low = (t_index // step) % 2 == 0
            moved = [jnp.where(low, x, y) for x, y in zip(moved, other)] + [
                jnp.where(low, y, x) for x, y in zip(moved, other)
            ]
            step *= 2
        full = jnp.concatenate(moved, axis=1)
        return jnp.einsum("aj,fbjk,ck->fbac", order, full, order, preferred_element_type=F32).astype(BF16)

    right_parts = right_factor[:, 0].reshape(loops, sections, 1, sub, size, size)
    left_parts = left_factor[:, 0].reshape(loops, sections, 1, sub, size, size)
    weights = []
    for loop in range(loops):
        if loop == 0:
            rights = scattered(right_parts[loop])
            lefts = scattered(left_parts[loop])
            weights.append((gathered(rights[0])[0], gathered(lefts[0])[0]))
            parts = [jnp.concatenate(pair) for pair in zip(rights[1:], lefts[1:])]
        else:
            parts = scattered(jnp.concatenate([right_parts[loop], left_parts[loop]], axis=1))
        for part in parts:
            full = gathered(part)
            weights.append((full[0], full[1]))

    current = split(enter(inputs))
    grad = split(enter(cotangent))
    stored = []
    for right, left in weights:
        columns = []
        following = []
        for acts in current:
            mixed = jnp.einsum("bjk,bjr->bkr", right, acts, preferred_element_type=F32).astype(BF16)
            columns.append(exchange(mixed))
        for acts, column in zip(current, columns):
            activated = jax.nn.silu(column.astype(F32)).astype(BF16)
            second = jnp.einsum("kbc,kbr->kcr", left, activated, preferred_element_type=F32).astype(BF16)
            following.append((acts.astype(F32) + exchange(second).astype(F32)).astype(BF16))
        stored.append((current, columns))
        current = following
    outputs = leave(merge(current))

    def summed(parts):
        step = 1
        while step < groups:
            pairs = parts.reshape((parts.shape[0] // 2, 2) + parts.shape[1:])
            bit = (t_index // step) % 2
            keep = lax.dynamic_index_in_dim(pairs, bit, 1, keepdims=False)
            give = lax.dynamic_index_in_dim(pairs, 1 - bit, 1, keepdims=False)
            got = lax.ppermute(give, "t", [(t, t ^ step) for t in range(groups)])
            parts = (keep.astype(F32) + got.astype(F32)).astype(BF16)
            step *= 2
        return parts[0]

    sums = [None] * layers
    for layer in reversed(range(layers)):
        right, left = weights[layer]
        right_term = 0.0
        left_term = 0.0
        following = []
        for acts, column, grad_out in zip(*stored[layer], grad):
            grad_columns = exchange(grad_out)
            wide = column.astype(F32)
            activated = jax.nn.silu(wide).astype(BF16)
            left_term += jnp.einsum("kbr,kcr->kbc", activated, grad_columns, preferred_element_type=F32)
            grad_act = jnp.einsum("kbc,kcr->kbr", left, grad_columns, preferred_element_type=F32)
            grad_mixed = exchange((grad_act * silu_slope(wide)).astype(BF16))
            right_term += jnp.einsum("bjr,bkr->bjk", acts, grad_mixed, preferred_element_type=F32)
            branch = jnp.einsum("bjk,bkr->bjr", right, grad_mixed, preferred_element_type=F32)
            following.append((grad_out.astype(F32) + branch).astype(BF16))
        grad = following
        terms = jnp.stack([right_term.astype(BF16), left_term.astype(BF16)])
        terms = jnp.einsum("aj,fbac,ck->fbjk", order, terms, order, preferred_element_type=F32).astype(BF16)
        if layer:
            grad, terms = lax.optimization_barrier((grad, terms))
            terms = terms.reshape(2, groups, sub, size, size).transpose(1, 0, 2, 3, 4)
            terms = terms.reshape(2 * own, size, size)
            terms = lax.psum_scatter(terms, "t", scatter_dimension=0, tiled=True)
            sums[layer] = terms.reshape(2, sub, size, size)
        else:
            sums[layer] = [summed(terms[f].reshape(groups, sub, size, size)) for f in range(2)]
        if layer + LAG < layers:
            grad, sums[layer + LAG] = lax.optimization_barrier((grad, sums[layer + LAG]))
    input_grad = leave(merge(grad))

    grads = []
    for factor in (1, 0):
        halves = []
        for loop in reversed(range(loops)):
            mine = jnp.stack([sums[loop * sections + section][factor] for section in range(sections)])
            halves.insert(0, jnp.stack(scattered(mine)).reshape(1, held, size, size))
        grads.insert(0, jnp.stack(halves).astype(F32))
    return (outputs, input_grad, grads[0], grads[1])


def solution(mesh):
    sections = mesh.shape["section"]
    peers = mesh.shape["block"] // GROUPS
    grouped = Mesh(mesh.devices.reshape(sections, GROUPS, peers), ("s", "t", "x"))
    acts = P("s", ("t", "x"), None)
    factor = P(None, "s", ("t", "x"), None, None)
    return jax.shard_map(
        body,
        mesh=grouped,
        in_specs=(acts, acts, factor, factor),
        out_specs=(acts, acts, factor, factor),
        check_vma=False,
    )
```

```python
import jax
import jax.numpy as jnp
from jax import lax
from jax.sharding import PartitionSpec as P

F32 = jnp.float32
BF16 = jnp.bfloat16
ALL = ("section", "block")
CHAINS = 2
LAG = 2


def swap(parts, axes):
    return lax.all_to_all(parts, axes, split_axis=0, concat_axis=0, tiled=True)


def silu_slope(values):
    sigmoid = jax.nn.sigmoid(values)
    return sigmoid * (1.0 + values * (1.0 - sigmoid))


def device_order(size, sections, peers):
    natural = jnp.arange(size).reshape(peers, sections, -1)
    order = natural.transpose(1, 0, 2).reshape(size)
    return (order[:, None] == jnp.arange(size)[None, :]).astype(BF16)


def exchange(values):
    own, full, rows = values.shape
    pieces = values.transpose(1, 0, 2).reshape(full // own, own, own, rows)
    moved = swap(pieces, ALL)
    return moved.transpose(1, 0, 2, 3).reshape(own, full, rows)


def body(inputs, cotangent, right_factor, left_factor):
    sections = lax.axis_size("section")
    peers = lax.axis_size("block")
    loops, _, held, size, _ = right_factor.shape
    rows = inputs.shape[2]
    own = held // sections
    layers = loops * sections
    order = device_order(size, sections, peers)

    def enter(acts):
        parts = swap(acts.reshape(sections, own, size, rows), "section")
        parts = parts.transpose(1, 2, 0, 3).reshape(own, size, sections * rows)
        return jnp.einsum("aj,bjr->bar", order, parts, preferred_element_type=F32).astype(BF16)

    def leave(acts):
        acts = jnp.einsum("aj,bar->bjr", order, acts, preferred_element_type=F32).astype(BF16)
        parts = acts.reshape(own, size, sections, rows).transpose(2, 0, 1, 3)
        return swap(parts, "section").reshape(1, held * size, rows)

    def split(acts):
        return jnp.split(acts, CHAINS, axis=2)

    def merge(chains):
        return jnp.concatenate(chains, axis=2)

    weights = []
    for loop in range(loops):
        parts = jnp.stack([right_factor[loop, 0], left_factor[loop, 0]])
        parts = parts.reshape(2, sections, own, size, size).transpose(1, 0, 2, 3, 4)
        moved = swap(parts, "section")
        for section in range(sections):
            full = jnp.einsum(
                "aj,fbjk,ck->fbac", order, moved[section], order, preferred_element_type=F32
            ).astype(BF16)
            weights.append((full[0], full[1]))

    current = split(enter(inputs))
    grad = split(enter(cotangent))
    stored = []
    for right, left in weights:
        columns = []
        following = []
        for acts in current:
            mixed = jnp.einsum("bjk,bjr->bkr", right, acts, preferred_element_type=F32).astype(BF16)
            columns.append(exchange(mixed))
        for acts, column in zip(current, columns):
            activated = jax.nn.silu(column.astype(F32)).astype(BF16)
            second = jnp.einsum("kbc,kbr->kcr", left, activated, preferred_element_type=F32).astype(BF16)
            following.append((acts.astype(F32) + exchange(second).astype(F32)).astype(BF16))
        stored.append((current, columns))
        current = following
    outputs = leave(merge(current))

    sums = [None] * layers
    for layer in reversed(range(layers)):
        right, left = weights[layer]
        right_term = 0.0
        left_term = 0.0
        following = []
        for acts, column, grad_out in zip(*stored[layer], grad):
            grad_columns = exchange(grad_out)
            wide = column.astype(F32)
            activated = jax.nn.silu(wide).astype(BF16)
            left_term += jnp.einsum("kbr,kcr->kbc", activated, grad_columns, preferred_element_type=F32)
            grad_act = jnp.einsum("kbc,kcr->kbr", left, grad_columns, preferred_element_type=F32)
            grad_mixed = exchange((grad_act * silu_slope(wide)).astype(BF16))
            right_term += jnp.einsum("bjr,bkr->bjk", acts, grad_mixed, preferred_element_type=F32)
            branch = jnp.einsum("bjk,bkr->bjr", right, grad_mixed, preferred_element_type=F32)
            following.append((grad_out.astype(F32) + branch).astype(BF16))
        grad = following
        terms = jnp.stack([right_term.astype(BF16), left_term.astype(BF16)])
        sums[layer] = jnp.einsum(
            "aj,fbac,ck->fbjk", order, terms, order, preferred_element_type=F32
        ).astype(BF16)
        if layer + LAG < layers:
            grad, sums[layer + LAG] = lax.optimization_barrier((grad, sums[layer + LAG]))
    input_grad = leave(merge(grad))

    halves = []
    for loop in range(loops):
        moved = swap(jnp.stack(sums[loop * sections : (loop + 1) * sections]), "section")
        halves.append(moved.transpose(1, 0, 2, 3, 4).reshape(2, 1, held, size, size).astype(F32))
    grads = jnp.stack(halves)
    return (outputs, input_grad, grads[:, 0], grads[:, 1])


def solution(mesh):
    acts = P("section", "block", None)
    factor = P(None, "section", "block", None, None)
    return jax.shard_map(
        body,
        mesh=mesh,
        in_specs=(acts, acts, factor, factor),
        out_specs=(acts, acts, factor, factor),
        check_vma=False,
    )
```

```python
import jax
import jax.numpy as jnp
from jax import lax
from jax.sharding import Mesh, PartitionSpec as P

F32 = jnp.float32
BF16 = jnp.bfloat16
WIDE = ("s", "x")
GROUPS = 2
STRETCH = 2


def silu_slope(values):
    sigmoid = jax.nn.sigmoid(values)
    return sigmoid * (1.0 + values * (1.0 - sigmoid))


def group_order(size, sections, groups, peers):
    natural = jnp.arange(size).reshape(groups, peers, sections, -1)
    order = natural.transpose(2, 1, 0, 3).reshape(size)
    return (order[:, None] == jnp.arange(size)[None, :]).astype(BF16)


def exchange(values):
    own, full, rows = values.shape
    pieces = values.transpose(1, 0, 2).reshape(full // own, own, own, rows)
    moved = lax.all_to_all(pieces, WIDE, split_axis=0, concat_axis=0, tiled=True)
    return moved.transpose(1, 0, 2, 3).reshape(own, full, rows)


def forward_layer(acts, factors):
    mixed = jnp.einsum("bjk,bjr->bkr", factors[0], acts, preferred_element_type=F32).astype(BF16)
    columns = exchange(mixed)
    activated = jax.nn.silu(columns.astype(F32)).astype(BF16)
    second = jnp.einsum("kbc,kbr->kcr", factors[1], activated, preferred_element_type=F32).astype(BF16)
    following = (acts.astype(F32) + exchange(second).astype(F32)).astype(BF16)
    return following, (acts, columns)


def backward_layer(grad, saved):
    factors, (acts, columns) = saved
    grad_columns = exchange(grad)
    wide = columns.astype(F32)
    activated = jax.nn.silu(wide).astype(BF16)
    left_term = jnp.einsum("kbr,kcr->kbc", activated, grad_columns, preferred_element_type=F32)
    grad_act = jnp.einsum("kbc,kcr->kbr", factors[1], grad_columns, preferred_element_type=F32)
    grad_mixed = exchange((grad_act * silu_slope(wide)).astype(BF16))
    right_term = jnp.einsum("bjr,bkr->bjk", acts, grad_mixed, preferred_element_type=F32)
    branch = jnp.einsum("bjk,bkr->bjr", factors[0], grad_mixed, preferred_element_type=F32)
    following = (grad.astype(F32) + branch).astype(BF16)
    return following, jnp.stack([right_term.astype(BF16), left_term.astype(BF16)])


def body(inputs, cotangent, right_factor, left_factor):
    sections = lax.axis_size("s")
    groups = lax.axis_size("t")
    peers = lax.axis_size("x")
    loops, _, held, size, _ = right_factor.shape
    rows = inputs.shape[2]
    sub = held // sections
    own = sub * groups
    layers = loops * sections
    micros = sections // groups
    s_index = lax.axis_index("s")
    t_index = lax.axis_index("t")
    line = (s_index % micros) * groups + t_index
    order = group_order(size, sections, groups, peers)

    def pick(parts, index):
        return lax.dynamic_index_in_dim(parts, index, 0, keepdims=False)

    def turned(parts, send_by, place_by, target):
        moved = []
        for mask in range(sections):
            pairs = [(s * groups + t, target(s, t, mask)) for s in range(sections) for t in range(groups)]
            moved.append(lax.ppermute(pick(parts, send_by ^ mask), ("s", "t"), pairs))
        moved = jnp.stack(moved)
        return jnp.stack([pick(moved, place_by ^ part) for part in range(sections)])

    def into(s, t, mask):
        return (((s % micros) * groups + t) ^ mask) * groups + s // micros

    def outof(s, t, mask):
        line_to = s ^ mask
        return (t * micros + line_to // groups) * groups + line_to % groups

    def enter(acts):
        parts = turned(acts.reshape(sections, sub, size, rows), line, s_index, into)
        parts = parts.reshape(micros, own, size, rows).transpose(1, 2, 0, 3)
        parts = parts.reshape(own, size, micros * rows)
        return jnp.einsum("aj,bjr->bar", order, parts, preferred_element_type=F32).astype(BF16)

    def leave(acts):
        acts = jnp.einsum("aj,bar->bjr", order, acts, preferred_element_type=F32).astype(BF16)
        parts = acts.reshape(own, size, micros, rows).transpose(2, 0, 1, 3)
        parts = turned(parts.reshape(sections, sub, size, rows), s_index, line, outof)
        return parts.reshape(1, held * size, rows)

    def scattered(parts):
        moved = [pick(parts, s_index)]
        for mask in range(1, sections):
            pairs = [(s, s ^ mask) for s in range(sections)]
            moved.append(lax.ppermute(pick(parts, s_index ^ mask), "s", pairs))
        moved = jnp.stack(moved)
        return jnp.stack([pick(moved, s_index ^ section) for section in range(sections)])

    def gathered(part):
        moved = [part]
        step = 1
        while step < groups:
            pairs = [(t, t ^ step) for t in range(groups)]
            other = [lax.ppermute(one, "t", pairs) for one in moved]
            low = (t_index // step) % 2 == 0
            moved = [jnp.where(low, x, y) for x, y in zip(moved, other)] + [
                jnp.where(low, y, x) for x, y in zip(moved, other)
            ]
            step *= 2
        return jnp.concatenate(moved, axis=2)

    def summed(terms):
        parts = terms.reshape(terms.shape[:2] + (groups, sub, size, size)).transpose(2, 0, 1, 3, 4, 5)
        step = 1
        while step < groups:
            pairs = [(t, t ^ step) for t in range(groups)]
            parts = parts.reshape((parts.shape[0] // 2, 2) + parts.shape[1:])
            bit = (t_index // step) % 2
            keep = lax.dynamic_index_in_dim(parts, bit, 1, keepdims=False)
            give = lax.dynamic_index_in_dim(parts, 1 - bit, 1, keepdims=False)
            parts = (keep.astype(F32) + lax.ppermute(give, "t", pairs).astype(F32)).astype(BF16)
            step *= 2
        return parts[0]

    def ordered(factors):
        return jnp.einsum("aj,lfbjk,ck->lfbac", order, factors, order, preferred_element_type=F32).astype(BF16)

    def unordered(terms):
        return jnp.einsum("aj,lfbac,ck->lfbjk", order, terms, order, preferred_element_type=F32).astype(BF16)

    both = jnp.stack([right_factor[:, 0], left_factor[:, 0]], axis=1)
    both = both.reshape(loops, 2, sections, sub, size, size).transpose(0, 2, 1, 3, 4, 5)
    stretches = layers // STRETCH
    arrived = [scattered(both[0])]

    def fetch(stretch):
        loop, start = divmod(stretch * STRETCH, sections)
        return gathered(arrived[loop][start : start + STRETCH])

    current = enter(inputs)
    stored = []
    weights = [ordered(fetch(0))]
    later, weights[0], cotangent = lax.optimization_barrier((both[1:], weights[0], cotangent))
    arrived.extend(scattered(later[loop]) for loop in range(loops - 1))
    for stretch in range(stretches):
        coming = fetch(stretch + 1) if stretch + 1 < stretches else None
        if stretch + 1 == stretches:
            current, cotangent = lax.optimization_barrier((current, cotangent))
            grad = enter(cotangent)
        current, saved = lax.scan(forward_layer, current, weights[stretch])
        stored.append(saved)
        if coming is not None:
            current, coming = lax.optimization_barrier((current, coming))
            weights.append(ordered(coming))
    outputs = leave(current)

    per_loop = stretches // loops

    def returned(loop):
        mine = jnp.concatenate(sums[loop * per_loop : (loop + 1) * per_loop])
        return scattered(mine).transpose(1, 0, 2, 3, 4).reshape(2, 1, held, size, size)

    sums = [None] * stretches
    halves = [None] * loops
    beside = {"outputs": outputs}
    for stretch in reversed(range(stretches)):
        grad, terms = lax.scan(backward_layer, grad, (weights[stretch], stored[stretch]), reverse=True)
        grad, terms, beside = lax.optimization_barrier((grad, terms, beside))
        outputs = beside.get("outputs", outputs)
        ready = beside.get("half")
        if "sum" in beside:
            sums[stretch + 1] = beside["sum"]
        beside = {"sum": summed(unordered(terms))}
        loop = (stretch + 1) // per_loop
        if (stretch + 1) % per_loop == 0 and loop < loops:
            beside["half"] = returned(loop)
            owed = loop
        if ready is not None:
            halves[owed] = ready
    sums[0] = beside["sum"]
    halves[0] = returned(0)
    input_grad = leave(grad)
    grads = jnp.stack(halves).astype(F32)
    return (outputs, input_grad, grads[:, 0], grads[:, 1])


def solution(mesh):
    sections = mesh.shape["section"]
    peers = mesh.shape["block"] // GROUPS
    grouped = Mesh(mesh.devices.reshape(sections, GROUPS, peers), ("s", "t", "x"))
    acts = P("s", ("t", "x"), None)
    factor = P(None, "s", ("t", "x"), None, None)
    return jax.shard_map(
        body,
        mesh=grouped,
        in_specs=(acts, acts, factor, factor),
        out_specs=(acts, acts, factor, factor),
        check_vma=False,
    )
```

```python
import jax
import jax.numpy as jnp
from jax import lax
from jax.sharding import Mesh, PartitionSpec as P

F32 = jnp.float32
BF16 = jnp.bfloat16
WIDE = ("s", "x")
GROUPS = 2
STRETCH = 2


def silu_slope(values):
    sigmoid = jax.nn.sigmoid(values)
    return sigmoid * (1.0 + values * (1.0 - sigmoid))


def group_order(size, sections, groups, peers):
    natural = jnp.arange(size).reshape(groups, peers, sections, -1)
    order = natural.transpose(2, 1, 0, 3).reshape(size)
    return (order[:, None] == jnp.arange(size)[None, :]).astype(BF16)


def exchange(values):
    own, full, rows = values.shape
    pieces = values.transpose(1, 0, 2).reshape(full // own, own, own, rows)
    moved = lax.all_to_all(pieces, WIDE, split_axis=0, concat_axis=0, tiled=True)
    return moved.transpose(1, 0, 2, 3).reshape(own, full, rows)


def forward_layer(acts, factors):
    mixed = jnp.einsum("bjk,bjr->bkr", factors[0], acts, preferred_element_type=F32).astype(BF16)
    columns = exchange(mixed)
    activated = jax.nn.silu(columns.astype(F32)).astype(BF16)
    second = jnp.einsum("kbc,kbr->kcr", factors[1], activated, preferred_element_type=F32).astype(BF16)
    following = (acts.astype(F32) + exchange(second).astype(F32)).astype(BF16)
    return following, (acts, columns)


def backward_layer(grad, saved):
    factors, (acts, columns) = saved
    grad_columns = exchange(grad)
    wide = columns.astype(F32)
    activated = jax.nn.silu(wide).astype(BF16)
    left_term = jnp.einsum("kbr,kcr->kbc", activated, grad_columns, preferred_element_type=F32)
    grad_act = jnp.einsum("kbc,kcr->kbr", factors[1], grad_columns, preferred_element_type=F32)
    grad_mixed = exchange((grad_act * silu_slope(wide)).astype(BF16))
    right_term = jnp.einsum("bjr,bkr->bjk", acts, grad_mixed, preferred_element_type=F32)
    branch = jnp.einsum("bjk,bkr->bjr", factors[0], grad_mixed, preferred_element_type=F32)
    following = (grad.astype(F32) + branch).astype(BF16)
    return following, jnp.stack([right_term.astype(BF16), left_term.astype(BF16)])


def body(inputs, cotangent, right_factor, left_factor):
    sections = lax.axis_size("s")
    groups = lax.axis_size("t")
    peers = lax.axis_size("x")
    loops, _, held, size, _ = right_factor.shape
    rows = inputs.shape[2]
    sub = held // sections
    own = sub * groups
    layers = loops * sections
    micros = sections // groups
    s_index = lax.axis_index("s")
    t_index = lax.axis_index("t")
    line = (s_index % micros) * groups + t_index
    order = group_order(size, sections, groups, peers)

    def pick(parts, index):
        return lax.dynamic_index_in_dim(parts, index, 0, keepdims=False)

    def turned(parts, send_by, place_by, target):
        moved = []
        for mask in range(sections):
            pairs = [(s * groups + t, target(s, t, mask)) for s in range(sections) for t in range(groups)]
            moved.append(lax.ppermute(pick(parts, send_by ^ mask), ("s", "t"), pairs))
        moved = jnp.stack(moved)
        return jnp.stack([pick(moved, place_by ^ part) for part in range(sections)])

    def into(s, t, mask):
        return (((s % micros) * groups + t) ^ mask) * groups + s // micros

    def outof(s, t, mask):
        line_to = s ^ mask
        return (t * micros + line_to // groups) * groups + line_to % groups

    def enter(acts):
        parts = turned(acts.reshape(sections, sub, size, rows), line, s_index, into)
        parts = parts.reshape(micros, own, size, rows).transpose(1, 2, 0, 3)
        parts = parts.reshape(own, size, micros * rows)
        return jnp.einsum("aj,bjr->bar", order, parts, preferred_element_type=F32).astype(BF16)

    def leave(acts):
        acts = jnp.einsum("aj,bar->bjr", order, acts, preferred_element_type=F32).astype(BF16)
        parts = acts.reshape(own, size, micros, rows).transpose(2, 0, 1, 3)
        parts = turned(parts.reshape(sections, sub, size, rows), s_index, line, outof)
        return parts.reshape(1, held * size, rows)

    def scattered(*kinds):
        moved = [jnp.stack([pick(parts, s_index) for parts in kinds])]
        for mask in range(1, sections):
            pairs = [(s, s ^ mask) for s in range(sections)]
            value = jnp.stack([pick(parts, s_index ^ mask) for parts in kinds])
            moved.append(lax.ppermute(value, "s", pairs))
        moved = jnp.stack(moved)
        return [pick(moved, s_index ^ section) for section in range(sections)]

    def gathered(part):
        moved = [part]
        step = 1
        while step < groups:
            pairs = [(t, t ^ step) for t in range(groups)]
            other = [lax.ppermute(one, "t", pairs) for one in moved]
            low = (t_index // step) % 2 == 0
            moved = [jnp.where(low, x, y) for x, y in zip(moved, other)] + [
                jnp.where(low, y, x) for x, y in zip(moved, other)
            ]
            step *= 2
        return jnp.concatenate(moved, axis=2)

    def summed(terms):
        parts = terms.reshape(terms.shape[:2] + (groups, sub, size, size)).transpose(2, 0, 1, 3, 4, 5)
        step = 1
        while step < groups:
            pairs = [(t, t ^ step) for t in range(groups)]
            parts = parts.reshape((parts.shape[0] // 2, 2) + parts.shape[1:])
            bit = (t_index // step) % 2
            keep = lax.dynamic_index_in_dim(parts, bit, 1, keepdims=False)
            give = lax.dynamic_index_in_dim(parts, 1 - bit, 1, keepdims=False)
            parts = (keep.astype(F32) + lax.ppermute(give, "t", pairs).astype(F32)).astype(BF16)
            step *= 2
        return parts[0]

    def ordered(factors):
        return jnp.einsum("aj,lfbjk,ck->lfbac", order, factors, order, preferred_element_type=F32).astype(BF16)

    def unordered(terms):
        return jnp.einsum("aj,lfbac,ck->lfbjk", order, terms, order, preferred_element_type=F32).astype(BF16)

    stretches = layers // STRETCH
    per_loop = stretches // loops
    rights = right_factor[:, 0].reshape(loops, sections, sub, size, size)
    lefts = left_factor[:, 0].reshape(loops, sections, sub, size, size)

    def part_of(arrived, stretch):
        start = stretch * STRETCH % sections
        return jnp.stack(arrived[start : start + STRETCH])

    arrived = scattered(rights[0], lefts[0])
    parts = [part_of(arrived, stretch) for stretch in range(per_loop)]
    current = enter(inputs)
    weights = [ordered(gathered(parts[0]))]
    later = (parts[1:], rights[1:], lefts[1:], cotangent)
    current, weights[0], later = lax.optimization_barrier((current, weights[0], later))
    parts[1:], rights, lefts, cotangent = later
    for loop in range(loops - 1):
        arrived = scattered(rights[loop], lefts[loop])
        parts.extend(part_of(arrived, stretch + loop * per_loop) for stretch in range(per_loop))
    stored = []
    for stretch in range(stretches):
        coming = None
        if stretch + 1 < stretches:
            coming = gathered(parts[stretch + 1])
        if stretch + 2 == stretches:
            current, cotangent = lax.optimization_barrier((current, cotangent))
            grad = enter(cotangent)
        current, saved = lax.scan(forward_layer, current, weights[stretch])
        stored.append(saved)
        if coming is not None:
            weights.append(ordered(coming))
    current, grad = lax.optimization_barrier((current, grad))

    def returned(loop):
        mine = jnp.concatenate(sums[loop * per_loop : (loop + 1) * per_loop])
        moved = jnp.stack(scattered(mine))
        return moved.reshape(sections, 2, sub, size, size).transpose(1, 0, 2, 3, 4).reshape(2, 1, held, size, size)

    sums = [None] * stretches
    halves = [None] * loops
    outputs = leave(current)
    for stretch in reversed(range(stretches)):
        grad, terms = lax.scan(backward_layer, grad, (weights[stretch], stored[stretch]), reverse=True)
        two_ago = sums[stretch + 2] if stretch + 2 < stretches else outputs
        if stretch + 1 < stretches:
            grad, terms, two_ago = lax.optimization_barrier((grad, terms, two_ago))
            if stretch + 2 < stretches:
                sums[stretch + 2] = two_ago
            else:
                outputs = two_ago
        sums[stretch] = summed(unordered(terms))
        loop = (stretch + 2) // per_loop
        if (stretch + 2) % per_loop == 0 and 0 < loop < loops:
            halves[loop] = returned(loop)
    halves[0] = returned(0)
    input_grad = leave(grad)
    grads = jnp.stack(halves).astype(F32)
    return (outputs, input_grad, grads[:, 0], grads[:, 1])


def solution(mesh):
    sections = mesh.shape["section"]
    peers = mesh.shape["block"] // GROUPS
    grouped = Mesh(mesh.devices.reshape(sections, GROUPS, peers), ("s", "t", "x"))
    acts = P("s", ("t", "x"), None)
    factor = P(None, "s", ("t", "x"), None, None)
    return jax.shard_map(
        body,
        mesh=grouped,
        in_specs=(acts, acts, factor, factor),
        out_specs=(acts, acts, factor, factor),
        check_vma=False,
    )
```

```python
import jax
import jax.numpy as jnp
from jax import lax
from jax.sharding import Mesh, PartitionSpec as P

F32 = jnp.float32
BF16 = jnp.bfloat16
WIDE = ("s", "x")
GROUPS = 4
STRETCH = 2


def silu_slope(values):
    sigmoid = jax.nn.sigmoid(values)
    return sigmoid * (1.0 + values * (1.0 - sigmoid))


def group_order(size, sections, groups, peers):
    natural = jnp.arange(size).reshape(groups, peers, sections, -1)
    order = natural.transpose(2, 1, 0, 3).reshape(size)
    return (order[:, None] == jnp.arange(size)[None, :]).astype(BF16)


def exchange(values):
    own, full, rows = values.shape
    pieces = values.transpose(1, 0, 2).reshape(full // own, own, own, rows)
    moved = lax.all_to_all(pieces, WIDE, split_axis=0, concat_axis=0, tiled=True)
    return moved.transpose(1, 0, 2, 3).reshape(own, full, rows)


def forward_layer(acts, factors):
    mixed = jnp.einsum("bjk,bjr->bkr", factors[0], acts, preferred_element_type=F32).astype(BF16)
    columns = exchange(mixed)
    activated = jax.nn.silu(columns.astype(F32)).astype(BF16)
    second = jnp.einsum("kbc,kbr->kcr", factors[1], activated, preferred_element_type=F32).astype(BF16)
    following = (acts.astype(F32) + exchange(second).astype(F32)).astype(BF16)
    return following, (acts, columns)


def backward_layer(grad, saved):
    factors, (acts, columns) = saved
    grad_columns = exchange(grad)
    wide = columns.astype(F32)
    activated = jax.nn.silu(wide).astype(BF16)
    left_term = jnp.einsum("kbr,kcr->kbc", activated, grad_columns, preferred_element_type=F32)
    grad_act = jnp.einsum("kbc,kcr->kbr", factors[1], grad_columns, preferred_element_type=F32)
    grad_mixed = exchange((grad_act * silu_slope(wide)).astype(BF16))
    right_term = jnp.einsum("bjr,bkr->bjk", acts, grad_mixed, preferred_element_type=F32)
    branch = jnp.einsum("bjk,bkr->bjr", factors[0], grad_mixed, preferred_element_type=F32)
    following = (grad.astype(F32) + branch).astype(BF16)
    return following, jnp.stack([right_term.astype(BF16), left_term.astype(BF16)])


def body(inputs, cotangent, right_factor, left_factor):
    sections = lax.axis_size("s")
    groups = lax.axis_size("t")
    peers = lax.axis_size("x")
    loops, _, held, size, _ = right_factor.shape
    rows = inputs.shape[2]
    sub = held // sections
    own = sub * groups
    layers = loops * sections
    micros = sections // groups
    s_index = lax.axis_index("s")
    t_index = lax.axis_index("t")
    line = (s_index % micros) * groups + t_index
    order = group_order(size, sections, groups, peers)

    def pick(parts, index):
        return lax.dynamic_index_in_dim(parts, index, 0, keepdims=False)

    def turned(parts, send_by, place_by, target):
        moved = []
        for mask in range(sections):
            pairs = [(s * groups + t, target(s, t, mask)) for s in range(sections) for t in range(groups)]
            moved.append(lax.ppermute(pick(parts, send_by ^ mask), ("s", "t"), pairs))
        moved = jnp.stack(moved)
        return jnp.stack([pick(moved, place_by ^ part) for part in range(sections)])

    def into(s, t, mask):
        return (((s % micros) * groups + t) ^ mask) * groups + s // micros

    def outof(s, t, mask):
        line_to = s ^ mask
        return (t * micros + line_to // groups) * groups + line_to % groups

    def enter(acts):
        parts = turned(acts.reshape(sections, sub, size, rows), line, s_index, into)
        parts = parts.reshape(micros, own, size, rows).transpose(1, 2, 0, 3)
        parts = parts.reshape(own, size, micros * rows)
        return jnp.einsum("aj,bjr->bar", order, parts, preferred_element_type=F32).astype(BF16)

    def leave(acts):
        acts = jnp.einsum("aj,bar->bjr", order, acts, preferred_element_type=F32).astype(BF16)
        parts = acts.reshape(own, size, micros, rows).transpose(2, 0, 1, 3)
        parts = turned(parts.reshape(sections, sub, size, rows), s_index, line, outof)
        return parts.reshape(1, held * size, rows)

    def scattered(*kinds):
        moved = [jnp.stack([pick(parts, s_index) for parts in kinds])]
        for mask in range(1, sections):
            pairs = [(s, s ^ mask) for s in range(sections)]
            value = jnp.stack([pick(parts, s_index ^ mask) for parts in kinds])
            moved.append(lax.ppermute(value, "s", pairs))
        moved = jnp.stack(moved)
        return [pick(moved, s_index ^ section) for section in range(sections)]

    def gathered(part):
        part = jnp.einsum("aj,lfbjk,ck->lfbac", order, part, order, preferred_element_type=F32).astype(BF16)
        full = lax.all_gather(part, "t", axis=0, tiled=False)
        return full.transpose(1, 2, 0, 3, 4, 5).reshape(part.shape[:2] + (own, size, size))

    def summed(terms):
        parts = terms.reshape(terms.shape[:2] + (groups, sub, size, size)).transpose(2, 0, 1, 3, 4, 5)
        total = lax.psum_scatter(parts.reshape(-1, size, size), "t", scatter_dimension=0, tiled=True)
        total = total.reshape(terms.shape[:2] + (sub, size, size))
        return jnp.einsum("aj,lfbac,ck->lfbjk", order, total, order, preferred_element_type=F32).astype(BF16)

    stretches = layers // STRETCH
    per_loop = stretches // loops
    rights = right_factor[:, 0].reshape(loops, sections, sub, size, size)
    lefts = left_factor[:, 0].reshape(loops, sections, sub, size, size)

    def part_of(arrived, stretch):
        start = stretch * STRETCH % sections
        return jnp.stack(arrived[start : start + STRETCH])

    arrived = scattered(rights[0], lefts[0])
    parts = [part_of(arrived, stretch) for stretch in range(per_loop)]
    current = enter(inputs)
    weights = [gathered(parts[0])]
    later = (parts[1:], rights[1:], lefts[1:], cotangent)
    current, weights[0], later = lax.optimization_barrier((current, weights[0], later))
    parts[1:], rights, lefts, cotangent = later
    for loop in range(loops - 1):
        arrived = scattered(rights[loop], lefts[loop])
        parts.extend(part_of(arrived, stretch + loop * per_loop) for stretch in range(per_loop))
    stored = []
    for stretch in range(stretches):
        coming = None
        if stretch + 1 < stretches:
            coming = gathered(parts[stretch + 1])
        if stretch + 2 == stretches:
            current, cotangent = lax.optimization_barrier((current, cotangent))
            grad = enter(cotangent)
        current, saved = lax.scan(forward_layer, current, weights[stretch])
        stored.append(saved)
        if coming is not None:
            weights.append(coming)
    current, grad = lax.optimization_barrier((current, grad))

    def returned(loop):
        mine = jnp.concatenate(sums[loop * per_loop : (loop + 1) * per_loop])
        moved = jnp.stack(scattered(mine))
        return moved.reshape(sections, 2, sub, size, size).transpose(1, 0, 2, 3, 4).reshape(2, 1, held, size, size)

    sums = [None] * stretches
    halves = [None] * loops
    outputs = leave(current)
    for stretch in reversed(range(stretches)):
        grad, terms = lax.scan(backward_layer, grad, (weights[stretch], stored[stretch]), reverse=True)
        two_ago = sums[stretch + 2] if stretch + 2 < stretches else outputs
        if stretch + 1 < stretches:
            grad, terms, two_ago = lax.optimization_barrier((grad, terms, two_ago))
            if stretch + 2 < stretches:
                sums[stretch + 2] = two_ago
            else:
                outputs = two_ago
        sums[stretch] = summed(terms)
        loop = (stretch + 2) // per_loop
        if (stretch + 2) % per_loop == 0 and 0 < loop < loops:
            halves[loop] = returned(loop)
    halves[0] = returned(0)
    input_grad = leave(grad)
    grads = jnp.stack(halves).astype(F32)
    return (outputs, input_grad, grads[:, 0], grads[:, 1])


def solution(mesh):
    sections = mesh.shape["section"]
    peers = mesh.shape["block"] // GROUPS
    grouped = Mesh(mesh.devices.reshape(sections, GROUPS, peers), ("s", "t", "x"))
    acts = P("s", ("t", "x"), None)
    factor = P(None, "s", ("t", "x"), None, None)
    return jax.shard_map(
        body,
        mesh=grouped,
        in_specs=(acts, acts, factor, factor),
        out_specs=(acts, acts, factor, factor),
        check_vma=False,
    )
```

```python
import jax
import jax.numpy as jnp
from jax import lax
from jax.sharding import Mesh, PartitionSpec as P

F32 = jnp.float32
BF16 = jnp.bfloat16
WIDE = ("s", "x")
GROUPS = 4
PAIRED = 2


def silu_slope(values):
    sigmoid = jax.nn.sigmoid(values)
    return sigmoid * (1.0 + values * (1.0 - sigmoid))


def group_order(size, sections, groups, peers):
    natural = jnp.arange(size).reshape(groups, peers, sections, -1)
    order = natural.transpose(2, 1, 0, 3).reshape(size)
    return (order[:, None] == jnp.arange(size)[None, :]).astype(BF16)


def exchange(values):
    own, full, rows = values.shape
    pieces = values.transpose(1, 0, 2).reshape(full // own, own, own, rows)
    moved = lax.all_to_all(pieces, WIDE, split_axis=0, concat_axis=0, tiled=True)
    return moved.transpose(1, 0, 2, 3).reshape(own, full, rows)


def forward_layer(acts, right, left):
    mixed = jnp.einsum("bjk,bjr->bkr", right, acts, preferred_element_type=F32).astype(BF16)
    columns = exchange(mixed)
    activated = jax.nn.silu(columns.astype(F32)).astype(BF16)
    second = jnp.einsum("kbc,kbr->kcr", left, activated, preferred_element_type=F32).astype(BF16)
    following = (acts.astype(F32) + exchange(second).astype(F32)).astype(BF16)
    return following, (acts, columns)


def backward_layer(grad, right, left, saved):
    acts, columns = saved
    grad_columns = exchange(grad)
    wide = columns.astype(F32)
    activated = jax.nn.silu(wide).astype(BF16)
    left_term = jnp.einsum("kbr,kcr->kbc", activated, grad_columns, preferred_element_type=F32)
    grad_act = jnp.einsum("kbc,kcr->kbr", left, grad_columns, preferred_element_type=F32)
    grad_mixed = exchange((grad_act * silu_slope(wide)).astype(BF16))
    right_term = jnp.einsum("bjr,bkr->bjk", acts, grad_mixed, preferred_element_type=F32)
    branch = jnp.einsum("bjk,bkr->bjr", right, grad_mixed, preferred_element_type=F32)
    following = (grad.astype(F32) + branch).astype(BF16)
    return following, right_term.astype(BF16), left_term.astype(BF16)


def body(inputs, cotangent, right_factor, left_factor):
    sections = lax.axis_size("s")
    groups = lax.axis_size("t")
    peers = lax.axis_size("x")
    loops, _, held, size, _ = right_factor.shape
    rows = inputs.shape[2]
    sub = held // sections
    own = sub * groups
    layers = loops * sections
    micros = sections // groups
    s_index = lax.axis_index("s")
    t_index = lax.axis_index("t")
    line = (s_index % micros) * groups + t_index
    order = group_order(size, sections, groups, peers)

    def pick(parts, index):
        return lax.dynamic_index_in_dim(parts, index, 0, keepdims=False)

    def turned(parts, send_by, place_by, target):
        moved = []
        for mask in range(sections):
            pairs = [(s * groups + t, target(s, t, mask)) for s in range(sections) for t in range(groups)]
            moved.append(lax.ppermute(pick(parts, send_by ^ mask), ("s", "t"), pairs))
        moved = jnp.stack(moved)
        return jnp.stack([pick(moved, place_by ^ part) for part in range(sections)])

    def into(s, t, mask):
        return (((s % micros) * groups + t) ^ mask) * groups + s // micros

    def outof(s, t, mask):
        line_to = s ^ mask
        return (t * micros + line_to // groups) * groups + line_to % groups

    def arriving(acts):
        parts = turned(acts.reshape(sections, sub, size, rows), line, s_index, into)
        parts = parts.reshape(micros, own, size, rows).transpose(1, 2, 0, 3)
        return parts.reshape(own, size, micros * rows)

    def settled(parts):
        return jnp.einsum("aj,bjr->bar", order, parts, preferred_element_type=F32).astype(BF16)

    def leave(acts):
        acts = jnp.einsum("aj,bar->bjr", order, acts, preferred_element_type=F32).astype(BF16)
        parts = acts.reshape(own, size, micros, rows).transpose(2, 0, 1, 3)
        parts = turned(parts.reshape(sections, sub, size, rows), s_index, line, outof)
        return parts.reshape(1, held * size, rows)

    def scattered(*kinds):
        moved = [jnp.stack([pick(parts, s_index) for parts in kinds])]
        for mask in range(1, sections):
            pairs = [(s, s ^ mask) for s in range(sections)]
            value = jnp.stack([pick(parts, s_index ^ mask) for parts in kinds])
            moved.append(lax.ppermute(value, "s", pairs))
        moved = jnp.stack(moved)
        return [pick(moved, s_index ^ section) for section in range(sections)]

    def ordered(part):
        return jnp.einsum("aj,fbjk,ck->fbac", order, part, order, preferred_element_type=F32).astype(BF16)

    def gathered(part):
        full = lax.all_gather(part, "t", axis=0, tiled=False)
        return [full[:, f].reshape(own, size, size) for f in range(part.shape[0])]

    def summed(terms):
        total = lax.psum_scatter(terms, "t", scatter_dimension=0, tiled=True)
        return jnp.einsum("aj,bac,ck->bjk", order, total, order, preferred_element_type=F32).astype(BF16)

    rights = right_factor[:, 0].reshape(loops, sections, sub, size, size)
    lefts = left_factor[:, 0].reshape(loops, sections, sub, size, size)
    parts = [ordered(part) for part in scattered(rights[0], lefts[0])]
    current = arriving(inputs)
    current, parts[0] = lax.optimization_barrier((current, parts[0]))
    weights = [(gathered(parts[0][:1])[0], gathered(parts[0][1:])[0])]
    later, weights[0] = lax.optimization_barrier(((rights[1:], lefts[1:], cotangent), weights[0]))
    rights, lefts, cotangent = later
    for loop in range(loops - 1):
        parts.extend(ordered(part) for part in scattered(rights[loop], lefts[loop]))

    current = settled(current)
    grad = settled(arriving(cotangent))
    stored = []
    for layer in range(layers):
        if layer + 1 < layers:
            current, parts[layer + 1] = lax.optimization_barrier((current, parts[layer + 1]))
            weights.append(tuple(gathered(parts[layer + 1])))
        current, saved = forward_layer(current, *weights[layer])
        stored.append(saved)
    outputs = leave(current)

    def returned(loop, factor):
        mine = jnp.stack([sums[loop * sections + section][factor] for section in range(sections)])
        return jnp.stack(scattered(mine)).reshape(1, held, size, size)

    once = 1 + s_index // sections
    sums = [None] * layers

    def backward_pair(first):
        def run(_, carry):
            grad, *factors = carry
            terms = []
            for step in range(PAIRED):
                right, left = factors[2 * step : 2 * step + 2]
                grad, right_term, left_term = backward_layer(grad, right, left, stored[first - step])
                terms += [right_term, left_term]
            return (grad, *terms)

        return run

    layer = layers - 1
    while layer >= PAIRED:
        factors = [factor for step in range(PAIRED) for factor in weights[layer - step]]
        grad, *terms = lax.fori_loop(0, once, backward_pair(layer), (grad, *factors))
        for step in range(PAIRED):
            sums[layer - step] = [summed(term) for term in terms[2 * step : 2 * step + 2]]
        layer -= PAIRED
    while layer >= 0:
        grad, right_term, left_term = backward_layer(grad, *weights[layer], stored[layer])
        sums[layer] = [summed(right_term), summed(left_term)]
        layer -= 1
    input_grad = leave(grad)
    halves = [jnp.stack([returned(loop, factor) for factor in range(2)]) for loop in range(loops)]
    grads = jnp.stack(halves).astype(F32)
    return (outputs, input_grad, grads[:, 0], grads[:, 1])


def solution(mesh):
    sections = mesh.shape["section"]
    peers = mesh.shape["block"] // GROUPS
    grouped = Mesh(mesh.devices.reshape(sections, GROUPS, peers), ("s", "t", "x"))
    acts = P("s", ("t", "x"), None)
    factor = P(None, "s", ("t", "x"), None, None)
    return jax.shard_map(
        body,
        mesh=grouped,
        in_specs=(acts, acts, factor, factor),
        out_specs=(acts, acts, factor, factor),
        check_vma=False,
    )
```

```python
import jax
import jax.numpy as jnp
from jax import lax
from jax.sharding import Mesh, PartitionSpec as P

F32 = jnp.float32
BF16 = jnp.bfloat16
WIDE = ("s", "x")
GROUPS = 4
PAIRED = 2


def silu_slope(values):
    sigmoid = jax.nn.sigmoid(values)
    return sigmoid * (1.0 + values * (1.0 - sigmoid))


def group_order(size, sections, groups, peers):
    natural = jnp.arange(size).reshape(groups, peers, sections, -1)
    order = natural.transpose(2, 1, 0, 3).reshape(size)
    return (order[:, None] == jnp.arange(size)[None, :]).astype(BF16)


def exchange(values):
    own, full, rows = values.shape
    pieces = values.transpose(1, 0, 2).reshape(full // own, own, own, rows)
    moved = lax.all_to_all(pieces, WIDE, split_axis=0, concat_axis=0, tiled=True)
    return moved.transpose(1, 0, 2, 3).reshape(own, full, rows)


def forward_layer(acts, right, left):
    mixed = jnp.einsum("bjk,bjr->bkr", right, acts, preferred_element_type=F32).astype(BF16)
    columns = exchange(mixed)
    activated = jax.nn.silu(columns.astype(F32)).astype(BF16)
    second = jnp.einsum("kbc,kbr->kcr", left, activated, preferred_element_type=F32).astype(BF16)
    following = (acts.astype(F32) + exchange(second).astype(F32)).astype(BF16)
    return following, (acts, columns)


def backward_layer(grad, right, left, saved):
    acts, columns = saved
    grad_columns = exchange(grad)
    wide = columns.astype(F32)
    activated = jax.nn.silu(wide).astype(BF16)
    left_term = jnp.einsum("kbr,kcr->kbc", activated, grad_columns, preferred_element_type=F32)
    grad_act = jnp.einsum("kbc,kcr->kbr", left, grad_columns, preferred_element_type=F32)
    grad_mixed = exchange((grad_act * silu_slope(wide)).astype(BF16))
    right_term = jnp.einsum("bjr,bkr->bjk", acts, grad_mixed, preferred_element_type=F32)
    branch = jnp.einsum("bjk,bkr->bjr", right, grad_mixed, preferred_element_type=F32)
    following = (grad.astype(F32) + branch).astype(BF16)
    return following, right_term.astype(BF16), left_term.astype(BF16)


def body(inputs, cotangent, right_factor, left_factor):
    sections = lax.axis_size("s")
    groups = lax.axis_size("t")
    peers = lax.axis_size("x")
    loops, _, held, size, _ = right_factor.shape
    rows = inputs.shape[2]
    sub = held // sections
    own = sub * groups
    layers = loops * sections
    micros = sections // groups
    s_index = lax.axis_index("s")
    t_index = lax.axis_index("t")
    line = (s_index % micros) * groups + t_index
    order = group_order(size, sections, groups, peers)

    def pick(parts, index):
        return lax.dynamic_index_in_dim(parts, index, 0, keepdims=False)

    def turned(parts, send_by, place_by, target):
        moved = []
        for mask in range(sections):
            pairs = [(s * groups + t, target(s, t, mask)) for s in range(sections) for t in range(groups)]
            moved.append(lax.ppermute(pick(parts, send_by ^ mask), ("s", "t"), pairs))
        moved = jnp.stack(moved)
        return jnp.stack([pick(moved, place_by ^ part) for part in range(sections)])

    def into(s, t, mask):
        return (((s % micros) * groups + t) ^ mask) * groups + s // micros

    def outof(s, t, mask):
        line_to = s ^ mask
        return (t * micros + line_to // groups) * groups + line_to % groups

    def arriving(acts):
        parts = turned(acts.reshape(sections, sub, size, rows), line, s_index, into)
        parts = parts.reshape(micros, own, size, rows).transpose(1, 2, 0, 3)
        return parts.reshape(own, size, micros * rows)

    def settled(parts):
        return jnp.einsum("aj,bjr->bar", order, parts, preferred_element_type=F32).astype(BF16)

    def leave(acts):
        acts = jnp.einsum("aj,bar->bjr", order, acts, preferred_element_type=F32).astype(BF16)
        parts = acts.reshape(own, size, micros, rows).transpose(2, 0, 1, 3)
        parts = turned(parts.reshape(sections, sub, size, rows), s_index, line, outof)
        return parts.reshape(1, held * size, rows)

    def scattered(*kinds):
        moved = [jnp.stack([pick(parts, s_index) for parts in kinds])]
        for mask in range(1, sections):
            pairs = [(s, s ^ mask) for s in range(sections)]
            value = jnp.stack([pick(parts, s_index ^ mask) for parts in kinds])
            moved.append(lax.ppermute(value, "s", pairs))
        moved = jnp.stack(moved)
        return [pick(moved, s_index ^ section) for section in range(sections)]

    def ordered(part):
        return jnp.einsum("aj,fbjk,ck->fbac", order, part, order, preferred_element_type=F32).astype(BF16)

    def gathered(part):
        full = lax.all_gather(part, "t", axis=0, tiled=False)
        return [full[:, f].reshape(own, size, size) for f in range(part.shape[0])]

    def around(value_of):
        moved = [value_of(0)]
        for mask in range(1, groups):
            moved.append(lax.ppermute(value_of(mask), "t", [(t, t ^ mask) for t in range(groups)]))
        return moved

    def gathered_directly(part):
        moved = jnp.stack(around(lambda mask: part))
        return jnp.concatenate([pick(moved, t_index ^ group) for group in range(groups)])

    def unordered(total):
        return jnp.einsum("aj,fbac,ck->fbjk", order, total, order, preferred_element_type=F32).astype(BF16)

    def summed(terms):
        total = lax.psum_scatter(terms.reshape(-1, size, size), "t", scatter_dimension=0, tiled=True)
        return unordered(total.reshape(terms.shape[1:]))

    def summed_directly(term):
        parts = term.reshape(groups, sub, size, size)
        moved = around(lambda mask: pick(parts, t_index ^ mask))
        return unordered(sum(one.astype(F32) for one in moved).astype(BF16)[None])

    def laid_out(*terms):
        return jnp.stack([term.reshape(groups, sub, size, size) for term in terms], axis=1)

    rights = right_factor[:, 0].reshape(loops, sections, sub, size, size)
    lefts = left_factor[:, 0].reshape(loops, sections, sub, size, size)
    parts = [ordered(part) for part in scattered(rights[0], lefts[0])]
    current = arriving(inputs)
    current, parts[0] = lax.optimization_barrier((current, parts[0]))
    weights = [(gathered_directly(parts[0][0]), gathered_directly(parts[0][1]))]
    later, right = lax.optimization_barrier(((rights[1:], lefts[1:]), weights[0][0]))
    rights, lefts = later
    weights[0] = (right, weights[0][1])
    for loop in range(loops - 1):
        parts.extend(ordered(part) for part in scattered(rights[loop], lefts[loop]))

    current = settled(current)
    stored = []
    for layer in range(layers):
        if layer + 1 < layers:
            current, parts[layer + 1] = lax.optimization_barrier((current, parts[layer + 1]))
            weights.append(tuple(gathered(parts[layer + 1])))
        else:
            current, cotangent = lax.optimization_barrier((current, cotangent))
            grad = settled(arriving(cotangent))
        current, saved = forward_layer(current, *weights[layer])
        stored.append(saved)
    outputs = leave(current)

    once = 1 + s_index // sections
    sums = [None] * layers

    def backward_pair(first):
        def run(_, carry):
            grad, _ = carry
            terms = []
            for layer in range(first, first - PAIRED, -1):
                grad, *pair = backward_layer(grad, *weights[layer], stored[layer])
                terms += pair
            return grad, laid_out(*terms)

        return run

    layer = layers - 1
    while layer >= PAIRED:
        blank = jnp.zeros((groups, 2 * PAIRED, sub, size, size), BF16)
        grad, terms = lax.fori_loop(0, once, backward_pair(layer), (grad, blank))
        total = summed(terms)
        for step in range(PAIRED):
            sums[layer - step] = [total[2 * step], total[2 * step + 1]]
        layer -= PAIRED
    while layer >= 0:
        grad, right_term, left_term = backward_layer(grad, *weights[layer], stored[layer])
        if layer:
            total = summed(laid_out(right_term, left_term))
            sums[layer] = [total[0], total[1]]
        else:
            sums[layer] = [summed_directly(right_term)[0], summed(laid_out(left_term))[0]]
        layer -= 1
    input_grad = leave(grad)

    def of_loop(loop, factor):
        return jnp.stack([sums[loop * sections + section][factor] for section in range(sections)])

    halves = []
    for loop in range(loops):
        if loop:
            moved = jnp.stack(scattered(of_loop(loop, 0), of_loop(loop, 1)), axis=1)
        else:
            moved = jnp.stack([jnp.stack(scattered(of_loop(loop, factor)))[:, 0] for factor in range(2)])
        halves.append(moved.reshape(2, 1, held, size, size))
    grads = jnp.stack(halves).astype(F32)
    return (outputs, input_grad, grads[:, 0], grads[:, 1])


def solution(mesh):
    sections = mesh.shape["section"]
    peers = mesh.shape["block"] // GROUPS
    grouped = Mesh(mesh.devices.reshape(sections, GROUPS, peers), ("s", "t", "x"))
    acts = P("s", ("t", "x"), None)
    factor = P(None, "s", ("t", "x"), None, None)
    return jax.shard_map(
        body,
        mesh=grouped,
        in_specs=(acts, acts, factor, factor),
        out_specs=(acts, acts, factor, factor),
        check_vma=False,
    )
```

```python
import jax
import jax.numpy as jnp
from jax import lax
from jax.sharding import Mesh, PartitionSpec as P

F32 = jnp.float32
BF16 = jnp.bfloat16
WIDE = ("s", "x")
GROUPS = 4
PAIRED = 2


def silu_slope(values):
    sigmoid = jax.nn.sigmoid(values)
    return sigmoid * (1.0 + values * (1.0 - sigmoid))


def group_order(size, sections, groups, peers):
    natural = jnp.arange(size).reshape(groups, peers, sections, -1)
    order = natural.transpose(2, 1, 0, 3).reshape(size)
    return (order[:, None] == jnp.arange(size)[None, :]).astype(BF16)


def exchange(values):
    own, full, rows = values.shape
    pieces = values.transpose(1, 0, 2).reshape(full // own, own, own, rows)
    moved = lax.all_to_all(pieces, WIDE, split_axis=0, concat_axis=0, tiled=True)
    return moved.transpose(1, 0, 2, 3).reshape(own, full, rows)


def forward_layer(acts, right, left):
    mixed = jnp.einsum("bjk,bjr->bkr", right, acts, preferred_element_type=F32).astype(BF16)
    columns = exchange(mixed)
    activated = jax.nn.silu(columns.astype(F32)).astype(BF16)
    second = jnp.einsum("kbc,kbr->kcr", left, activated, preferred_element_type=F32).astype(BF16)
    following = (acts.astype(F32) + exchange(second).astype(F32)).astype(BF16)
    return following, (acts, columns)


def backward_layer(grad, right, left, saved):
    acts, columns = saved
    grad_columns = exchange(grad)
    wide = columns.astype(F32)
    activated = jax.nn.silu(wide).astype(BF16)
    left_term = jnp.einsum("kbr,kcr->kbc", activated, grad_columns, preferred_element_type=F32)
    grad_act = jnp.einsum("kbc,kcr->kbr", left, grad_columns, preferred_element_type=F32)
    grad_mixed = exchange((grad_act * silu_slope(wide)).astype(BF16))
    right_term = jnp.einsum("bjr,bkr->bjk", acts, grad_mixed, preferred_element_type=F32)
    branch = jnp.einsum("bjk,bkr->bjr", right, grad_mixed, preferred_element_type=F32)
    following = (grad.astype(F32) + branch).astype(BF16)
    return following, right_term.astype(BF16), left_term.astype(BF16)


def body(inputs, cotangent, right_factor, left_factor):
    sections = lax.axis_size("s")
    groups = lax.axis_size("t")
    peers = lax.axis_size("x")
    loops, _, held, size, _ = right_factor.shape
    rows = inputs.shape[2]
    sub = held // sections
    own = sub * groups
    layers = loops * sections
    micros = sections // groups
    s_index = lax.axis_index("s")
    t_index = lax.axis_index("t")
    line = (s_index % micros) * groups + t_index
    order = group_order(size, sections, groups, peers)

    def pick(parts, index):
        return lax.dynamic_index_in_dim(parts, index, 0, keepdims=False)

    def turned(parts, send_by, place_by, target):
        moved = []
        for mask in range(sections):
            pairs = [(s * groups + t, target(s, t, mask)) for s in range(sections) for t in range(groups)]
            moved.append(lax.ppermute(pick(parts, send_by ^ mask), ("s", "t"), pairs))
        moved = jnp.stack(moved)
        return jnp.stack([pick(moved, place_by ^ part) for part in range(sections)])

    def into(s, t, mask):
        return (((s % micros) * groups + t) ^ mask) * groups + s // micros

    def outof(s, t, mask):
        line_to = s ^ mask
        return (t * micros + line_to // groups) * groups + line_to % groups

    def arriving(acts):
        parts = turned(acts.reshape(sections, sub, size, rows), line, s_index, into)
        parts = parts.reshape(micros, own, size, rows).transpose(1, 2, 0, 3)
        return parts.reshape(own, size, micros * rows)

    def settled(parts):
        return jnp.einsum("aj,bjr->bar", order, parts, preferred_element_type=F32).astype(BF16)

    def leave(acts):
        acts = jnp.einsum("aj,bar->bjr", order, acts, preferred_element_type=F32).astype(BF16)
        parts = acts.reshape(own, size, micros, rows).transpose(2, 0, 1, 3)
        parts = turned(parts.reshape(sections, sub, size, rows), s_index, line, outof)
        return parts.reshape(1, held * size, rows)

    def scattered(*kinds):
        moved = [jnp.stack([pick(parts, s_index) for parts in kinds])]
        for mask in range(1, sections):
            pairs = [(s, s ^ mask) for s in range(sections)]
            value = jnp.stack([pick(parts, s_index ^ mask) for parts in kinds])
            moved.append(lax.ppermute(value, "s", pairs))
        moved = jnp.stack(moved)
        return [pick(moved, s_index ^ section) for section in range(sections)]

    def ordered(part):
        return jnp.einsum("aj,fbjk,ck->fbac", order, part, order, preferred_element_type=F32).astype(BF16)

    def gathered(part):
        return lax.all_gather(part, "t", axis=0, tiled=False)

    def pair_of(full):
        return [full[:, f].reshape(own, size, size) for f in range(2)]

    def around(value_of):
        moved = [value_of(0)]
        for mask in range(1, groups):
            moved.append(lax.ppermute(value_of(mask), "t", [(t, t ^ mask) for t in range(groups)]))
        return moved

    def gathered_directly(part):
        moved = jnp.stack(around(lambda mask: part))
        return jnp.stack([pick(moved, t_index ^ group) for group in range(groups)])

    def unordered(total):
        return jnp.einsum("aj,fbac,ck->fbjk", order, total, order, preferred_element_type=F32).astype(BF16)

    def summed(terms):
        total = lax.psum_scatter(terms.reshape(-1, size, size), "t", scatter_dimension=0, tiled=True)
        return unordered(total.reshape(terms.shape[1:]))

    def laid_out(*terms):
        return jnp.stack([term.reshape(groups, sub, size, size) for term in terms], axis=1)

    rights = right_factor[:, 0].reshape(loops, sections, sub, size, size)
    lefts = left_factor[:, 0].reshape(loops, sections, sub, size, size)
    parts = [ordered(part) for part in scattered(rights[0], lefts[0])]
    current = arriving(inputs)
    current, parts[0] = lax.optimization_barrier((current, parts[0]))
    first = [gathered_directly(parts[0][f]) for f in range(2)]
    later, first[0] = lax.optimization_barrier(((rights[1:], lefts[1:]), first[0]))
    rights, lefts = later
    weights = [jnp.stack(first, axis=1)]
    for loop in range(loops - 1):
        parts.extend(ordered(part) for part in scattered(rights[loop], lefts[loop]))

    current = settled(current)
    kept = [jnp.zeros((layers, own, size, micros * rows), BF16) for _ in range(2)]
    for layer in range(layers):
        if layer + 1 < layers:
            current, parts[layer + 1] = lax.optimization_barrier((current, parts[layer + 1]))
            weights.append(gathered(parts[layer + 1]))
        else:
            current, cotangent = lax.optimization_barrier((current, cotangent))
            grad = settled(arriving(cotangent))
        factors = pair_of(weights[layer]) if layer else [one.reshape(own, size, size) for one in first]
        current, saved = forward_layer(current, *factors)
        kept = [lax.dynamic_update_index_in_dim(all_of, one, layer, 0) for all_of, one in zip(kept, saved)]
        current, kept = lax.optimization_barrier((current, kept))
    outputs = leave(current)

    once = 1 + s_index // sections
    sums = [None] * layers

    def backward_pair(top):
        def run(_, carry):
            grad, _ = carry
            terms = []
            for layer in range(top, top - PAIRED, -1):
                saved = [all_of[layer] for all_of in kept]
                grad, *pair = backward_layer(grad, *pair_of(weights[layer]), saved)
                terms += pair
            return grad, laid_out(*terms)

        return run

    totals = {}
    for top in range(layers - 1, 0, -PAIRED):
        blank = jnp.zeros((groups, 2 * PAIRED, sub, size, size), BF16)
        grad, terms = lax.fori_loop(0, once, backward_pair(top), (grad, blank))
        if top + 2 * PAIRED in totals:
            asked = totals[top + 2 * PAIRED]
            grad, terms, totals[top + 2 * PAIRED] = lax.optimization_barrier((grad, terms, asked))
        totals[top] = summed(terms)
    for top, total in totals.items():
        for step in range(PAIRED):
            sums[top - step] = [total[2 * step], total[2 * step + 1]]
    input_grad = leave(grad)

    def of_loop(loop, factor):
        return jnp.stack([sums[loop * sections + section][factor] for section in range(sections)])

    halves = []
    for loop in range(loops):
        if loop:
            moved = jnp.stack(scattered(of_loop(loop, 0), of_loop(loop, 1)), axis=1)
        else:
            moved = jnp.stack([jnp.stack(scattered(of_loop(loop, factor)))[:, 0] for factor in range(2)])
        halves.append(moved.reshape(2, 1, held, size, size))
    grads = jnp.stack(halves).astype(F32)
    return (outputs, input_grad, grads[:, 0], grads[:, 1])


def solution(mesh):
    sections = mesh.shape["section"]
    peers = mesh.shape["block"] // GROUPS
    grouped = Mesh(mesh.devices.reshape(sections, GROUPS, peers), ("s", "t", "x"))
    acts = P("s", ("t", "x"), None)
    factor = P(None, "s", ("t", "x"), None, None)
    return jax.shard_map(
        body,
        mesh=grouped,
        in_specs=(acts, acts, factor, factor),
        out_specs=(acts, acts, factor, factor),
        check_vma=False,
    )
```

```python
import jax
import jax.numpy as jnp
from jax import lax
from jax.sharding import Mesh, PartitionSpec as P

F32 = jnp.float32
BF16 = jnp.bfloat16
WIDE = ("s", "x")
GROUPS = 4
PAIRED = 2


def silu_slope(values):
    sigmoid = jax.nn.sigmoid(values)
    return sigmoid * (1.0 + values * (1.0 - sigmoid))


def group_order(size, sections, groups, peers):
    natural = jnp.arange(size).reshape(groups, peers, sections, -1)
    order = natural.transpose(2, 1, 0, 3).reshape(size)
    return (order[:, None] == jnp.arange(size)[None, :]).astype(BF16)


def exchange(values):
    own, full, rows = values.shape
    pieces = values.transpose(1, 0, 2).reshape(full // own, own, own, rows)
    moved = lax.all_to_all(pieces, WIDE, split_axis=0, concat_axis=0, tiled=True)
    return moved.transpose(1, 0, 2, 3).reshape(own, full, rows)


def forward_layer(acts, right, left):
    mixed = jnp.einsum("bjk,bjr->bkr", right, acts, preferred_element_type=F32).astype(BF16)
    columns = exchange(mixed)
    activated = jax.nn.silu(columns.astype(F32)).astype(BF16)
    second = jnp.einsum("kbc,kbr->kcr", left, activated, preferred_element_type=F32).astype(BF16)
    following = (acts.astype(F32) + exchange(second).astype(F32)).astype(BF16)
    return following, (acts, columns)


def backward_layer(grad, right, left, saved):
    acts, columns = saved
    grad_columns = exchange(grad)
    wide = columns.astype(F32)
    activated = jax.nn.silu(wide).astype(BF16)
    left_term = jnp.einsum("kbr,kcr->kbc", activated, grad_columns, preferred_element_type=F32)
    grad_act = jnp.einsum("kbc,kcr->kbr", left, grad_columns, preferred_element_type=F32)
    grad_mixed = exchange((grad_act * silu_slope(wide)).astype(BF16))
    right_term = jnp.einsum("bjr,bkr->bjk", acts, grad_mixed, preferred_element_type=F32)
    branch = jnp.einsum("bjk,bkr->bjr", right, grad_mixed, preferred_element_type=F32)
    following = (grad.astype(F32) + branch).astype(BF16)
    return following, right_term.astype(BF16), left_term.astype(BF16)


def body(inputs, cotangent, right_factor, left_factor):
    sections = lax.axis_size("s")
    groups = lax.axis_size("t")
    peers = lax.axis_size("x")
    loops, _, held, size, _ = right_factor.shape
    rows = inputs.shape[2]
    sub = held // sections
    own = sub * groups
    layers = loops * sections
    micros = sections // groups
    s_index = lax.axis_index("s")
    t_index = lax.axis_index("t")
    line = (s_index % micros) * groups + t_index
    order = group_order(size, sections, groups, peers)

    def pick(parts, index):
        return lax.dynamic_index_in_dim(parts, index, 0, keepdims=False)

    def turned(parts, send_by, place_by, target):
        moved = []
        for mask in range(sections):
            pairs = [(s * groups + t, target(s, t, mask)) for s in range(sections) for t in range(groups)]
            moved.append(lax.ppermute(pick(parts, send_by ^ mask), ("s", "t"), pairs))
        moved = jnp.stack(moved)
        return jnp.stack([pick(moved, place_by ^ part) for part in range(sections)])

    def into(s, t, mask):
        return (((s % micros) * groups + t) ^ mask) * groups + s // micros

    def outof(s, t, mask):
        line_to = s ^ mask
        return (t * micros + line_to // groups) * groups + line_to % groups

    def arriving(acts):
        parts = turned(acts.reshape(sections, sub, size, rows), line, s_index, into)
        parts = parts.reshape(micros, own, size, rows).transpose(1, 2, 0, 3)
        return parts.reshape(own, size, micros * rows)

    def settled(parts):
        return jnp.einsum("aj,bjr->bar", order, parts, preferred_element_type=F32).astype(BF16)

    def unsettled(acts):
        return jnp.einsum("aj,bar->bjr", order, acts, preferred_element_type=F32).astype(BF16)

    def leave(acts):
        parts = acts.reshape(own, size, micros, rows).transpose(2, 0, 1, 3)
        parts = turned(parts.reshape(sections, sub, size, rows), s_index, line, outof)
        return parts.reshape(1, held * size, rows)

    def scattered(*kinds):
        moved = [jnp.stack([pick(parts, s_index) for parts in kinds])]
        for mask in range(1, sections):
            pairs = [(s, s ^ mask) for s in range(sections)]
            value = jnp.stack([pick(parts, s_index ^ mask) for parts in kinds])
            moved.append(lax.ppermute(value, "s", pairs))
        moved = jnp.stack(moved)
        return [pick(moved, s_index ^ section) for section in range(sections)]

    def ordered(part):
        return jnp.einsum("aj,fbjk,ck->fbac", order, part, order, preferred_element_type=F32).astype(BF16)

    def gathered(part):
        return lax.all_gather(part, "t", axis=0, tiled=False)

    def around(value_of):
        moved = [value_of(0)]
        for mask in range(1, groups):
            moved.append(lax.ppermute(value_of(mask), "t", [(t, t ^ mask) for t in range(groups)]))
        return moved

    def gathered_directly(part):
        moved = jnp.stack(around(lambda mask: part))
        return jnp.stack([pick(moved, t_index ^ group) for group in range(groups)])

    def unordered(total):
        return jnp.einsum("aj,fbac,ck->fbjk", order, total, order, preferred_element_type=F32).astype(BF16)

    def summed(terms):
        total = lax.psum_scatter(terms.reshape(-1, size, size), "t", scatter_dimension=0, tiled=True)
        return unordered(total.reshape(terms.shape[1:]))

    def laid_out(*terms):
        return jnp.stack([term.reshape(groups, sub, size, size) for term in terms], axis=1)

    rights = right_factor[:, 0].reshape(loops, sections, sub, size, size)
    lefts = left_factor[:, 0].reshape(loops, sections, sub, size, size)
    parts = [ordered(part) for part in scattered(rights[0], lefts[0])]
    current = arriving(inputs)
    current, parts[0] = lax.optimization_barrier((current, parts[0]))
    once = 1 + s_index // sections
    first = jnp.stack([gathered_directly(parts[0][f]) for f in range(2)], axis=1)[:, None]
    starts = [0, 1] + list(range(PAIRED, layers, PAIRED)) + [layers]
    ahead = gathered(jnp.stack(parts[1:2]))
    weights = {}
    stored = {}
    current = settled(current)

    def factors_of(layer):
        full, step = weights[layer]
        return [full[:, step, f].reshape(own, size, size) for f in range(2)]

    def forward_stretch(stretch):
        def run(_, carry):
            acts = carry[0]
            saved = []
            for layer in stretch:
                acts, pair = forward_layer(acts, *factors_of(layer))
                saved += pair
            return (acts, *saved[1:])

        return run

    for begin, end in zip(starts, starts[1:]):
        stretch = range(begin, end)
        full = ahead if begin else first
        if begin:
            coming = range(end, min(end + PAIRED, layers))
            if begin == 1:
                current, rights, lefts = lax.optimization_barrier((current, rights[1:], lefts[1:]))
                for loop in range(loops - 1):
                    parts.extend(ordered(part) for part in scattered(rights[loop], lefts[loop]))
            if coming:
                ahead = gathered(jnp.stack([parts[layer] for layer in coming]))
        weights.update((layer, (full, layer - begin)) for layer in stretch)
        if end + PAIRED == layers:
            current, cotangent = lax.optimization_barrier((current, cotangent))
            grad = settled(arriving(cotangent))
        blanks = [jnp.zeros(current.shape, BF16) for _ in range(2 * len(stretch) - 1)]
        entered = current
        current, *saved = lax.fori_loop(0, once, forward_stretch(stretch), (current, *blanks))
        saved = [entered] + saved
        stored.update((layer, saved[2 * step : 2 * step + 2]) for step, layer in enumerate(stretch))
    outputs = leave(unsettled(current))

    sums = [None] * layers

    def backward_pair(top):
        def run(_, carry):
            grad, _ = carry
            terms = []
            for layer in range(top, top - PAIRED, -1):
                grad, *pair = backward_layer(grad, *factors_of(layer), stored[layer])
                terms += pair
            return grad, laid_out(*terms)

        return run

    totals = {}
    for top in range(layers - 1, 0, -PAIRED):
        blank = jnp.zeros((groups, 2 * PAIRED, sub, size, size), BF16)
        grad, terms = lax.fori_loop(0, once, backward_pair(top), (grad, blank))
        if top + 2 * PAIRED in totals:
            asked = totals[top + 2 * PAIRED]
            grad, terms, totals[top + 2 * PAIRED] = lax.optimization_barrier((grad, terms, asked))
        totals[top] = summed(terms)
    grad = lax.fori_loop(0, once, lambda _, acts: unsettled(acts), grad)
    if 2 * PAIRED <= layers:
        grad, totals[2 * PAIRED - 1] = lax.optimization_barrier((grad, totals[2 * PAIRED - 1]))
    for top, total in totals.items():
        for step in range(PAIRED):
            sums[top - step] = [total[2 * step], total[2 * step + 1]]
    input_grad = leave(grad)

    def of_loop(loop, factor):
        return jnp.stack([sums[loop * sections + section][factor] for section in range(sections)])

    halves = []
    for loop in range(loops):
        if loop:
            moved = jnp.stack(scattered(of_loop(loop, 0), of_loop(loop, 1)), axis=1)
        else:
            moved = jnp.stack([jnp.stack(scattered(of_loop(loop, factor)))[:, 0] for factor in range(2)])
        halves.append(moved.reshape(2, 1, held, size, size))
    grads = jnp.stack(halves).astype(F32)
    return (outputs, input_grad, grads[:, 0], grads[:, 1])


def solution(mesh):
    sections = mesh.shape["section"]
    peers = mesh.shape["block"] // GROUPS
    grouped = Mesh(mesh.devices.reshape(sections, GROUPS, peers), ("s", "t", "x"))
    acts = P("s", ("t", "x"), None)
    factor = P(None, "s", ("t", "x"), None, None)
    return jax.shard_map(
        body,
        mesh=grouped,
        in_specs=(acts, acts, factor, factor),
        out_specs=(acts, acts, factor, factor),
        check_vma=False,
    )
```

```python
import jax
import jax.numpy as jnp
from jax import lax
from jax.sharding import Mesh, PartitionSpec as P

F32 = jnp.float32
BF16 = jnp.bfloat16
WIDE = ("s", "x")
GROUPS = 4
PAIRED = 2


def silu_slope(values):
    sigmoid = jax.nn.sigmoid(values)
    return sigmoid * (1.0 + values * (1.0 - sigmoid))


def group_order(size, sections, groups, peers):
    natural = jnp.arange(size).reshape(groups, peers, sections, -1)
    order = natural.transpose(2, 1, 0, 3).reshape(size)
    return (order[:, None] == jnp.arange(size)[None, :]).astype(BF16)


def exchange(values):
    own, full, rows = values.shape
    pieces = values.transpose(1, 0, 2).reshape(full // own, own, own, rows)
    moved = lax.all_to_all(pieces, WIDE, split_axis=0, concat_axis=0, tiled=True)
    return moved.transpose(1, 0, 2, 3).reshape(own, full, rows)


def forward_layer(acts, right, left):
    mixed = jnp.einsum("bjk,bjr->bkr", right, acts, preferred_element_type=F32).astype(BF16)
    columns = exchange(mixed)
    activated = jax.nn.silu(columns.astype(F32)).astype(BF16)
    second = jnp.einsum("kbc,kbr->kcr", left, activated, preferred_element_type=F32).astype(BF16)
    following = (acts.astype(F32) + exchange(second).astype(F32)).astype(BF16)
    return following, (acts, columns)


def backward_layer(grad, right, left, saved):
    acts, columns = saved
    grad_columns = exchange(grad)
    wide = columns.astype(F32)
    activated = jax.nn.silu(wide).astype(BF16)
    left_term = jnp.einsum("kbr,kcr->kbc", activated, grad_columns, preferred_element_type=F32)
    grad_act = jnp.einsum("kbc,kcr->kbr", left, grad_columns, preferred_element_type=F32)
    grad_mixed = exchange((grad_act * silu_slope(wide)).astype(BF16))
    right_term = jnp.einsum("bjr,bkr->bjk", acts, grad_mixed, preferred_element_type=F32)
    branch = jnp.einsum("bjk,bkr->bjr", right, grad_mixed, preferred_element_type=F32)
    following = (grad.astype(F32) + branch).astype(BF16)
    return following, right_term.astype(BF16), left_term.astype(BF16)


def body(inputs, cotangent, right_factor, left_factor):
    sections = lax.axis_size("s")
    groups = lax.axis_size("t")
    peers = lax.axis_size("x")
    loops, _, held, size, _ = right_factor.shape
    rows = inputs.shape[2]
    sub = held // sections
    own = sub * groups
    layers = loops * sections
    micros = sections // groups
    s_index = lax.axis_index("s")
    t_index = lax.axis_index("t")
    line = (s_index % micros) * groups + t_index
    order = group_order(size, sections, groups, peers)

    def pick(parts, index):
        return lax.dynamic_index_in_dim(parts, index, 0, keepdims=False)

    def turned(parts, send_by, place_by, target):
        moved = []
        for mask in range(sections):
            pairs = [(s * groups + t, target(s, t, mask)) for s in range(sections) for t in range(groups)]
            moved.append(lax.ppermute(pick(parts, send_by ^ mask), ("s", "t"), pairs))
        moved = jnp.stack(moved)
        return jnp.stack([pick(moved, place_by ^ part) for part in range(sections)])

    def into(s, t, mask):
        return (((s % micros) * groups + t) ^ mask) * groups + s // micros

    def outof(s, t, mask):
        line_to = s ^ mask
        return (t * micros + line_to // groups) * groups + line_to % groups

    def arriving(acts):
        parts = turned(acts.reshape(sections, sub, size, rows), line, s_index, into)
        parts = parts.reshape(micros, own, size, rows).transpose(1, 2, 0, 3)
        return parts.reshape(own, size, micros * rows)

    def settled(parts):
        return jnp.einsum("aj,bjr->bar", order, parts, preferred_element_type=F32).astype(BF16)

    def unsettled(acts):
        return jnp.einsum("aj,bar->bjr", order, acts, preferred_element_type=F32).astype(BF16)

    def leave(acts):
        parts = acts.reshape(own, size, micros, rows).transpose(2, 0, 1, 3)
        parts = turned(parts.reshape(sections, sub, size, rows), s_index, line, outof)
        return parts.reshape(1, held * size, rows)

    def scattered(*kinds):
        moved = [jnp.stack([pick(parts, s_index) for parts in kinds])]
        for mask in range(1, sections):
            pairs = [(s, s ^ mask) for s in range(sections)]
            value = jnp.stack([pick(parts, s_index ^ mask) for parts in kinds])
            moved.append(lax.ppermute(value, "s", pairs))
        moved = jnp.stack(moved)
        return [pick(moved, s_index ^ section) for section in range(sections)]

    def ordered(part):
        return jnp.einsum("aj,fbjk,ck->fbac", order, part, order, preferred_element_type=F32).astype(BF16)

    def gathered(part):
        return lax.all_gather(part, "t", axis=0, tiled=False)

    def around(value_of):
        moved = [value_of(0)]
        for mask in range(1, groups):
            moved.append(lax.ppermute(value_of(mask), "t", [(t, t ^ mask) for t in range(groups)]))
        return moved

    def gathered_directly(part):
        moved = jnp.stack(around(lambda mask: part))
        return jnp.stack([pick(moved, t_index ^ group) for group in range(groups)])

    def unordered(total):
        return jnp.einsum("aj,fbac,ck->fbjk", order, total, order, preferred_element_type=F32).astype(BF16)

    def summed(terms):
        total = lax.psum_scatter(terms.reshape(-1, size, size), "t", scatter_dimension=0, tiled=True)
        return unordered(total.reshape(terms.shape[1:]))

    def laid_out(*terms):
        return jnp.stack([term.reshape(groups, sub, size, size) for term in terms], axis=1)

    rights = right_factor[:, 0].reshape(loops, sections, sub, size, size)
    lefts = left_factor[:, 0].reshape(loops, sections, sub, size, size)
    parts = [ordered(part) for part in scattered(rights[0], lefts[0])]
    current = arriving(inputs)
    current, parts[0] = lax.optimization_barrier((current, parts[0]))
    once = 1 + s_index // sections
    first = jnp.stack([gathered_directly(parts[0][f]) for f in range(2)], axis=1)[:, None]
    starts = [0, 1] + list(range(PAIRED, layers, PAIRED)) + [layers]
    first, parts[1] = lax.optimization_barrier((first, parts[1]))
    ahead = gathered(jnp.stack(parts[1:2]))
    weights = {}
    stored = {}
    current = settled(current)

    def factors_of(layer):
        full, step = weights[layer]
        return [full[:, step, f].reshape(own, size, size) for f in range(2)]

    def forward_stretch(stretch):
        def run(_, carry):
            acts = carry[0]
            saved = []
            for layer in stretch:
                acts, pair = forward_layer(acts, *factors_of(layer))
                saved += pair
            return (acts, *saved[1:])

        return run

    for begin, end in zip(starts, starts[1:]):
        stretch = range(begin, end)
        full = ahead if begin else first
        if begin:
            coming = range(end, min(end + PAIRED, layers))
            if begin == PAIRED:
                later = (current, rights[1:], lefts[1:], cotangent)
                current, rights, lefts, cotangent = lax.optimization_barrier(later)
                for loop in range(loops - 1):
                    parts.extend(ordered(part) for part in scattered(rights[loop], lefts[loop]))
                grad = settled(arriving(cotangent))
            if coming:
                ahead = gathered(jnp.stack([parts[layer] for layer in coming]))
        weights.update((layer, (full, layer - begin)) for layer in stretch)
        blanks = [jnp.zeros(current.shape, BF16) for _ in range(2 * len(stretch) - 1)]
        entered = current
        current, *saved = lax.fori_loop(0, once, forward_stretch(stretch), (current, *blanks))
        saved = [entered] + saved
        stored.update((layer, saved[2 * step : 2 * step + 2]) for step, layer in enumerate(stretch))
    outputs = leave(unsettled(current))

    sums = [None] * layers

    def backward_stretch(stretch):
        def run(_, carry):
            grad, _ = carry
            terms = []
            for layer in stretch:
                grad, *pair = backward_layer(grad, *factors_of(layer), stored[layer])
                terms += pair
            return grad, laid_out(*terms)

        return run

    backward = [range(end - 1, begin - 1, -1) for begin, end in zip(starts, starts[1:])][::-1]
    totals = []
    for place, stretch in enumerate(backward):
        blank = jnp.zeros((groups, 2 * len(stretch), sub, size, size), BF16)
        grad, terms = lax.fori_loop(0, once, backward_stretch(stretch), (grad, blank))
        if place >= 2 and len(stretch) == PAIRED:
            grad, terms, totals[place - 2] = lax.optimization_barrier((grad, terms, totals[place - 2]))
        totals.append(summed(terms))
    grad = lax.fori_loop(0, once, lambda _, acts: unsettled(acts), grad)
    grad, totals[1:-1] = lax.optimization_barrier((grad, totals[1:-1]))
    for stretch, total in zip(backward, totals):
        for step, layer in enumerate(stretch):
            sums[layer] = [total[2 * step], total[2 * step + 1]]
    input_grad = leave(grad)

    def of_loop(loop, factor):
        return jnp.stack([sums[loop * sections + section][factor] for section in range(sections)])

    halves = []
    for loop in range(loops):
        moved = jnp.stack(scattered(of_loop(loop, 0), of_loop(loop, 1)), axis=1)
        halves.append(moved.reshape(2, 1, held, size, size))
    grads = jnp.stack(halves).astype(F32)
    return (outputs, input_grad, grads[:, 0], grads[:, 1])


def solution(mesh):
    sections = mesh.shape["section"]
    peers = mesh.shape["block"] // GROUPS
    grouped = Mesh(mesh.devices.reshape(sections, GROUPS, peers), ("s", "t", "x"))
    acts = P("s", ("t", "x"), None)
    factor = P(None, "s", ("t", "x"), None, None)
    return jax.shard_map(
        body,
        mesh=grouped,
        in_specs=(acts, acts, factor, factor),
        out_specs=(acts, acts, factor, factor),
        check_vma=False,
    )
```

```python
import jax
import jax.numpy as jnp
from jax import lax
from jax.sharding import Mesh, PartitionSpec as P

F32 = jnp.float32
BF16 = jnp.bfloat16
WIDE = ("s", "x")
GROUPS = 4
PAIRED = 2


def silu_slope(values):
    sigmoid = jax.nn.sigmoid(values)
    return sigmoid * (1.0 + values * (1.0 - sigmoid))


def group_order(size, sections, groups, peers):
    natural = jnp.arange(size).reshape(groups, peers, sections, -1)
    order = natural.transpose(2, 1, 0, 3).reshape(size)
    return (order[:, None] == jnp.arange(size)[None, :]).astype(BF16)


def exchange(values):
    own, full, rows = values.shape
    pieces = values.transpose(1, 0, 2).reshape(full // own, own, own, rows)
    moved = lax.all_to_all(pieces, WIDE, split_axis=0, concat_axis=0, tiled=True)
    return moved.transpose(1, 0, 2, 3).reshape(own, full, rows)


def forward_layer(acts, right, left):
    mixed = jnp.einsum("bjk,bjr->bkr", right, acts, preferred_element_type=F32).astype(BF16)
    columns = exchange(mixed)
    activated = jax.nn.silu(columns.astype(F32)).astype(BF16)
    second = jnp.einsum("kbc,kbr->kcr", left, activated, preferred_element_type=F32).astype(BF16)
    following = (acts.astype(F32) + exchange(second).astype(F32)).astype(BF16)
    return following, (acts, columns)


def backward_layer(grad, right, left, saved):
    acts, columns = saved
    grad_columns = exchange(grad)
    wide = columns.astype(F32)
    activated = jax.nn.silu(wide).astype(BF16)
    left_term = jnp.einsum("kbr,kcr->kbc", activated, grad_columns, preferred_element_type=F32)
    grad_act = jnp.einsum("kbc,kcr->kbr", left, grad_columns, preferred_element_type=F32)
    grad_mixed = exchange((grad_act * silu_slope(wide)).astype(BF16))
    right_term = jnp.einsum("bjr,bkr->bjk", acts, grad_mixed, preferred_element_type=F32)
    branch = jnp.einsum("bjk,bkr->bjr", right, grad_mixed, preferred_element_type=F32)
    following = (grad.astype(F32) + branch).astype(BF16)
    return following, right_term.astype(BF16), left_term.astype(BF16)


def body(inputs, cotangent, right_factor, left_factor):
    sections = lax.axis_size("s")
    groups = lax.axis_size("t")
    peers = lax.axis_size("x")
    loops, _, held, size, _ = right_factor.shape
    rows = inputs.shape[2]
    sub = held // sections
    own = sub * groups
    layers = loops * sections
    micros = sections // groups
    s_index = lax.axis_index("s")
    t_index = lax.axis_index("t")
    line = (s_index % micros) * groups + t_index
    order = group_order(size, sections, groups, peers)

    def pick(parts, index):
        return lax.dynamic_index_in_dim(parts, index, 0, keepdims=False)

    def turned(parts, send_by, place_by, target):
        moved = []
        for mask in range(sections):
            pairs = [(s * groups + t, target(s, t, mask)) for s in range(sections) for t in range(groups)]
            moved.append(lax.ppermute(pick(parts, send_by ^ mask), ("s", "t"), pairs))
        moved = jnp.stack(moved)
        return jnp.stack([pick(moved, place_by ^ part) for part in range(sections)])

    def into(s, t, mask):
        return (((s % micros) * groups + t) ^ mask) * groups + s // micros

    def outof(s, t, mask):
        line_to = s ^ mask
        return (t * micros + line_to // groups) * groups + line_to % groups

    def arriving(acts):
        parts = turned(acts.reshape(sections, sub, size, rows), line, s_index, into)
        parts = parts.reshape(micros, own, size, rows).transpose(1, 2, 0, 3)
        return parts.reshape(own, size, micros * rows)

    def settled(parts):
        return jnp.einsum("aj,bjr->bar", order, parts, preferred_element_type=F32).astype(BF16)

    def unsettled(acts):
        return jnp.einsum("aj,bar->bjr", order, acts, preferred_element_type=F32).astype(BF16)

    def leave(acts):
        parts = acts.reshape(own, size, micros, rows).transpose(2, 0, 1, 3)
        parts = turned(parts.reshape(sections, sub, size, rows), s_index, line, outof)
        return parts.reshape(1, held * size, rows)

    def scattered(*kinds):
        moved = [jnp.stack([pick(parts, s_index) for parts in kinds])]
        for mask in range(1, sections):
            pairs = [(s, s ^ mask) for s in range(sections)]
            value = jnp.stack([pick(parts, s_index ^ mask) for parts in kinds])
            moved.append(lax.ppermute(value, "s", pairs))
        moved = jnp.stack(moved)
        return [pick(moved, s_index ^ section) for section in range(sections)]

    def ordered(part):
        return jnp.einsum("aj,fbjk,ck->fbac", order, part, order, preferred_element_type=F32).astype(BF16)

    def gathered(part):
        return lax.all_gather(part, "t", axis=0, tiled=False)

    def around(value_of):
        moved = [value_of(0)]
        for mask in range(1, groups):
            moved.append(lax.ppermute(value_of(mask), "t", [(t, t ^ mask) for t in range(groups)]))
        return moved

    def gathered_directly(part):
        moved = jnp.stack(around(lambda mask: part))
        return jnp.stack([pick(moved, t_index ^ group) for group in range(groups)])

    def unordered(total):
        return jnp.einsum("aj,fbac,ck->fbjk", order, total, order, preferred_element_type=F32).astype(BF16)

    def summed(terms):
        total = lax.psum_scatter(terms.reshape(-1, size, size), "t", scatter_dimension=0, tiled=True)
        return unordered(total.reshape(terms.shape[1:]))

    def laid_out(*terms):
        return jnp.stack([term.reshape(groups, sub, size, size) for term in terms], axis=1)

    rights = right_factor[:, 0].reshape(loops, sections, sub, size, size)
    lefts = left_factor[:, 0].reshape(loops, sections, sub, size, size)
    parts = [ordered(part) for part in scattered(rights[0], lefts[0])]
    current = arriving(inputs)
    current, parts[0] = lax.optimization_barrier((current, parts[0]))
    once = 1 + s_index // sections
    first = jnp.stack([gathered_directly(parts[0][f]) for f in range(2)], axis=1)[:, None]
    starts = [0, 1] + list(range(PAIRED, layers, PAIRED)) + [layers]
    first, parts[1] = lax.optimization_barrier((first, parts[1]))
    ahead = gathered(jnp.stack(parts[1:2]))
    weights = {}
    stored = {}
    current = settled(current)

    def factors_of(layer):
        full, step = weights[layer]
        return [full[:, step, f].reshape(own, size, size) for f in range(2)]

    def forward_stretch(stretch):
        def run(_, carry):
            acts = carry[0]
            saved = []
            for layer in stretch:
                acts, pair = forward_layer(acts, *factors_of(layer))
                saved += pair
            return (acts, *saved[1:])

        return run

    for begin, end in zip(starts, starts[1:]):
        stretch = range(begin, end)
        full = ahead if begin else first
        if begin:
            coming = range(end, min(end + PAIRED, layers))
            if begin == PAIRED:
                later = (current, rights[1:], lefts[1:], cotangent)
                current, rights, lefts, cotangent = lax.optimization_barrier(later)
                for loop in range(loops - 1):
                    parts.extend(ordered(part) for part in scattered(rights[loop], lefts[loop]))
                grad = settled(arriving(cotangent))
                grad, parts[end:] = lax.optimization_barrier((grad, parts[end:]))
            if coming:
                ahead = gathered(jnp.stack([parts[layer] for layer in coming]))
        weights.update((layer, (full, layer - begin)) for layer in stretch)
        blanks = [jnp.zeros(current.shape, BF16) for _ in range(2 * len(stretch) - 1)]
        entered = current
        current, *saved = lax.fori_loop(0, once, forward_stretch(stretch), (current, *blanks))
        saved = [entered] + saved
        stored.update((layer, saved[2 * step : 2 * step + 2]) for step, layer in enumerate(stretch))
    outputs = leave(unsettled(current))

    sums = [None] * layers

    def backward_stretch(stretch):
        def run(_, carry):
            grad = carry[0]
            terms = []
            for layer in stretch:
                grad, *pair = backward_layer(grad, *factors_of(layer), stored[layer])
                terms += pair
            return (grad, *terms)

        return run

    backward = [range(top, top - PAIRED, -1) for top in range(layers - 1, 0, -PAIRED)]
    totals = []
    for place, stretch in enumerate(backward):
        blanks = [jnp.zeros((own, size, size), BF16) for _ in range(2 * PAIRED)]
        grad, *terms = lax.fori_loop(0, once, backward_stretch(stretch), (grad, *blanks))
        if place >= 2:
            grad, terms, totals[place - 2] = lax.optimization_barrier((grad, terms, totals[place - 2]))
        totals.append(summed(laid_out(*terms)))
    grad = lax.fori_loop(0, once, lambda _, acts: unsettled(acts), grad)
    if len(totals) > 1:
        grad, totals[-2] = lax.optimization_barrier((grad, totals[-2]))
    for stretch, total in zip(backward, totals):
        for step, layer in enumerate(stretch):
            sums[layer] = [total[2 * step], total[2 * step + 1]]
    input_grad = leave(grad)

    def of_loop(loop, factor):
        return jnp.stack([sums[loop * sections + section][factor] for section in range(sections)])

    halves = []
    for loop in range(loops):
        moved = jnp.stack(scattered(of_loop(loop, 0), of_loop(loop, 1)), axis=1)
        halves.append(moved.reshape(2, 1, held, size, size))
    grads = jnp.stack(halves).astype(F32)
    return (outputs, input_grad, grads[:, 0], grads[:, 1])


def solution(mesh):
    sections = mesh.shape["section"]
    peers = mesh.shape["block"] // GROUPS
    grouped = Mesh(mesh.devices.reshape(sections, GROUPS, peers), ("s", "t", "x"))
    acts = P("s", ("t", "x"), None)
    factor = P(None, "s", ("t", "x"), None, None)
    return jax.shard_map(
        body,
        mesh=grouped,
        in_specs=(acts, acts, factor, factor),
        out_specs=(acts, acts, factor, factor),
        check_vma=False,
    )
```

```python
import jax
import jax.numpy as jnp
from jax import lax
from jax.sharding import Mesh, PartitionSpec as P

F32 = jnp.float32
BF16 = jnp.bfloat16
WIDE = ("s", "x")
GROUPS = 4
PAIRED = 2


def silu_slope(values):
    sigmoid = jax.nn.sigmoid(values)
    return sigmoid * (1.0 + values * (1.0 - sigmoid))


def group_order(size, sections, groups, peers):
    natural = jnp.arange(size).reshape(groups, peers, sections, -1)
    order = natural.transpose(2, 1, 0, 3).reshape(size)
    return (order[:, None] == jnp.arange(size)[None, :]).astype(BF16)


def exchange(values):
    own, full, rows = values.shape
    pieces = values.transpose(1, 0, 2).reshape(full // own, own, own, rows)
    moved = lax.all_to_all(pieces, WIDE, split_axis=0, concat_axis=0, tiled=True)
    return moved.transpose(1, 0, 2, 3).reshape(own, full, rows)


def forward_layer(acts, right, left):
    mixed = jnp.einsum("bjk,bjr->bkr", right, acts, preferred_element_type=F32).astype(BF16)
    columns = exchange(mixed)
    activated = jax.nn.silu(columns.astype(F32)).astype(BF16)
    second = jnp.einsum("kbc,kbr->kcr", left, activated, preferred_element_type=F32).astype(BF16)
    following = (acts.astype(F32) + exchange(second).astype(F32)).astype(BF16)
    return following, (acts, columns)


def backward_layer(grad, right, left, saved):
    acts, columns = saved
    grad_columns = exchange(grad)
    wide = columns.astype(F32)
    activated = jax.nn.silu(wide).astype(BF16)
    left_term = jnp.einsum("kbr,kcr->kbc", activated, grad_columns, preferred_element_type=F32)
    grad_act = jnp.einsum("kbc,kcr->kbr", left, grad_columns, preferred_element_type=F32)
    grad_mixed = exchange((grad_act * silu_slope(wide)).astype(BF16))
    right_term = jnp.einsum("bjr,bkr->bjk", acts, grad_mixed, preferred_element_type=F32)
    branch = jnp.einsum("bjk,bkr->bjr", right, grad_mixed, preferred_element_type=F32)
    following = (grad.astype(F32) + branch).astype(BF16)
    return following, right_term.astype(BF16), left_term.astype(BF16)


def body(inputs, cotangent, right_factor, left_factor):
    sections = lax.axis_size("s")
    groups = lax.axis_size("t")
    peers = lax.axis_size("x")
    loops, _, held, size, _ = right_factor.shape
    rows = inputs.shape[2]
    sub = held // sections
    own = sub * groups
    layers = loops * sections
    micros = sections // groups
    s_index = lax.axis_index("s")
    t_index = lax.axis_index("t")
    line = (s_index % micros) * groups + t_index
    order = group_order(size, sections, groups, peers)

    def pick(parts, index):
        return lax.dynamic_index_in_dim(parts, index, 0, keepdims=False)

    def turned(parts, send_by, place_by, target):
        moved = []
        for mask in range(sections):
            pairs = [(s * groups + t, target(s, t, mask)) for s in range(sections) for t in range(groups)]
            moved.append(lax.ppermute(pick(parts, send_by ^ mask), ("s", "t"), pairs))
        moved = jnp.stack(moved)
        return jnp.stack([pick(moved, place_by ^ part) for part in range(sections)])

    def into(s, t, mask):
        return (((s % micros) * groups + t) ^ mask) * groups + s // micros

    def outof(s, t, mask):
        line_to = s ^ mask
        return (t * micros + line_to // groups) * groups + line_to % groups

    def arriving(acts):
        parts = turned(acts.reshape(sections, sub, size, rows), line, s_index, into)
        parts = parts.reshape(micros, own, size, rows).transpose(1, 2, 0, 3)
        return parts.reshape(own, size, micros * rows)

    def settled(parts):
        return jnp.einsum("aj,bjr->bar", order, parts, preferred_element_type=F32).astype(BF16)

    def unsettled(acts):
        return jnp.einsum("aj,bar->bjr", order, acts, preferred_element_type=F32).astype(BF16)

    def leave(acts):
        parts = acts.reshape(own, size, micros, rows).transpose(2, 0, 1, 3)
        parts = turned(parts.reshape(sections, sub, size, rows), s_index, line, outof)
        return parts.reshape(1, held * size, rows)

    def scattered(*kinds):
        moved = [jnp.stack([pick(parts, s_index) for parts in kinds])]
        for mask in range(1, sections):
            pairs = [(s, s ^ mask) for s in range(sections)]
            value = jnp.stack([pick(parts, s_index ^ mask) for parts in kinds])
            moved.append(lax.ppermute(value, "s", pairs))
        moved = jnp.stack(moved)
        return [pick(moved, s_index ^ section) for section in range(sections)]

    def ordered(part):
        return jnp.einsum("aj,fbjk,ck->fbac", order, part, order, preferred_element_type=F32).astype(BF16)

    def gathered(part):
        return lax.all_gather(part, "t", axis=0, tiled=False)

    def around(value_of):
        moved = [value_of(0)]
        for mask in range(1, groups):
            moved.append(lax.ppermute(value_of(mask), "t", [(t, t ^ mask) for t in range(groups)]))
        return moved

    def gathered_directly(part):
        moved = jnp.stack(around(lambda mask: part))
        return jnp.stack([pick(moved, t_index ^ group) for group in range(groups)])

    def unordered(total):
        return jnp.einsum("aj,fbac,ck->fbjk", order, total, order, preferred_element_type=F32).astype(BF16)

    def summed(terms):
        total = lax.psum_scatter(terms.reshape(-1, size, size), "t", scatter_dimension=0, tiled=True)
        return unordered(total.reshape(terms.shape[1:]))

    def laid_out(*terms):
        return jnp.stack([term.reshape(groups, sub, size, size) for term in terms], axis=1)

    rights = right_factor[:, 0].reshape(loops, sections, sub, size, size)
    lefts = left_factor[:, 0].reshape(loops, sections, sub, size, size)
    parts = [ordered(part) for part in scattered(rights[0], lefts[0])]
    current = arriving(inputs)
    current, parts[0] = lax.optimization_barrier((current, parts[0]))
    once = 1 + s_index // sections
    parts[0], rights, lefts = lax.optimization_barrier((parts[0], rights[1:], lefts[1:]))
    for loop in range(loops - 1):
        parts.extend(ordered(part) for part in scattered(rights[loop], lefts[loop]))
    first = jnp.stack([gathered_directly(parts[0][f]) for f in range(2)], axis=1)[:, None]
    starts = [0, 1] + list(range(PAIRED, layers, PAIRED)) + [layers]
    ahead = gathered(jnp.stack(parts[1:2]))
    weights = {}
    stored = {}
    current = settled(current)

    def factors_of(layer):
        full, step = weights[layer]
        return [full[:, step, f].reshape(own, size, size) for f in range(2)]

    def forward_stretch(stretch):
        def run(_, carry):
            acts = carry[0]
            saved = []
            for layer in stretch:
                acts, pair = forward_layer(acts, *factors_of(layer))
                saved += pair
            return (acts, *saved[1:])

        return run

    for begin, end in zip(starts, starts[1:]):
        stretch = range(begin, end)
        full = ahead if begin else first
        if begin:
            coming = range(end, min(end + PAIRED, layers))
            if coming:
                ahead = gathered(jnp.stack([parts[layer] for layer in coming]))
        weights.update((layer, (full, layer - begin)) for layer in stretch)
        blanks = [jnp.zeros(current.shape, BF16) for _ in range(2 * len(stretch) - 1)]
        entered = current
        current, *saved = lax.fori_loop(0, once, forward_stretch(stretch), (current, *blanks))
        current, ahead = lax.optimization_barrier((current, ahead))
        saved = [entered] + saved
        stored.update((layer, saved[2 * step : 2 * step + 2]) for step, layer in enumerate(stretch))
    current, cotangent = lax.optimization_barrier((current, cotangent))
    grad = settled(arriving(cotangent))
    outputs = leave(unsettled(current))

    sums = [None] * layers

    def backward_pair(top):
        def run(_, carry):
            grad, _ = carry
            terms = []
            for layer in range(top, top - PAIRED, -1):
                grad, *pair = backward_layer(grad, *factors_of(layer), stored[layer])
                terms += pair
            return grad, laid_out(*terms)

        return run

    totals = {}
    for top in range(layers - 1, 0, -PAIRED):
        blank = jnp.zeros((groups, 2 * PAIRED, sub, size, size), BF16)
        grad, terms = lax.fori_loop(0, once, backward_pair(top), (grad, blank))
        if top + 2 * PAIRED in totals:
            asked = totals[top + 2 * PAIRED]
            grad, terms, totals[top + 2 * PAIRED] = lax.optimization_barrier((grad, terms, asked))
        totals[top] = summed(terms)
    grad = lax.fori_loop(0, once, lambda _, acts: unsettled(acts), grad)
    if 2 * PAIRED <= layers:
        grad, totals[2 * PAIRED - 1] = lax.optimization_barrier((grad, totals[2 * PAIRED - 1]))
    for top, total in totals.items():
        for step in range(PAIRED):
            sums[top - step] = [total[2 * step], total[2 * step + 1]]
    input_grad = leave(grad)

    def of_loop(loop, factor):
        return jnp.stack([sums[loop * sections + section][factor] for section in range(sections)])

    halves = []
    for loop in range(loops):
        moved = jnp.stack(scattered(of_loop(loop, 0), of_loop(loop, 1)), axis=1)
        halves.append(moved.reshape(2, 1, held, size, size))
    grads = jnp.stack(halves).astype(F32)
    return (outputs, input_grad, grads[:, 0], grads[:, 1])


def solution(mesh):
    sections = mesh.shape["section"]
    peers = mesh.shape["block"] // GROUPS
    grouped = Mesh(mesh.devices.reshape(sections, GROUPS, peers), ("s", "t", "x"))
    acts = P("s", ("t", "x"), None)
    factor = P(None, "s", ("t", "x"), None, None)
    return jax.shard_map(
        body,
        mesh=grouped,
        in_specs=(acts, acts, factor, factor),
        out_specs=(acts, acts, factor, factor),
        check_vma=False,
    )
```

```python
import jax
import jax.numpy as jnp
from jax import lax
from jax.sharding import Mesh, PartitionSpec as P

F32 = jnp.float32
BF16 = jnp.bfloat16
WIDE = ("s", "x")
GROUPS = 4
PAIRED = 2


def silu_slope(values):
    sigmoid = jax.nn.sigmoid(values)
    return sigmoid * (1.0 + values * (1.0 - sigmoid))


def group_order(size, sections, groups, peers):
    natural = jnp.arange(size).reshape(groups, peers, sections, -1)
    order = natural.transpose(2, 1, 0, 3).reshape(size)
    return (order[:, None] == jnp.arange(size)[None, :]).astype(BF16)


def exchange(values):
    own, full, rows = values.shape
    pieces = values.transpose(1, 0, 2).reshape(full // own, own, own, rows)
    moved = lax.all_to_all(pieces, WIDE, split_axis=0, concat_axis=0, tiled=True)
    return moved.transpose(1, 0, 2, 3).reshape(own, full, rows)


def forward_layer(acts, right, left):
    mixed = jnp.einsum("bjk,bjr->bkr", right, acts, preferred_element_type=F32).astype(BF16)
    columns = exchange(mixed)
    activated = jax.nn.silu(columns.astype(F32)).astype(BF16)
    second = jnp.einsum("kbc,kbr->kcr", left, activated, preferred_element_type=F32).astype(BF16)
    following = (acts.astype(F32) + exchange(second).astype(F32)).astype(BF16)
    return following, (acts, columns)


def backward_layer(grad, right, left, saved):
    acts, columns = saved
    grad_columns = exchange(grad)
    wide = columns.astype(F32)
    activated = jax.nn.silu(wide).astype(BF16)
    left_term = jnp.einsum("kbr,kcr->kbc", activated, grad_columns, preferred_element_type=F32)
    grad_act = jnp.einsum("kbc,kcr->kbr", left, grad_columns, preferred_element_type=F32)
    grad_mixed = exchange((grad_act * silu_slope(wide)).astype(BF16))
    right_term = jnp.einsum("bjr,bkr->bjk", acts, grad_mixed, preferred_element_type=F32)
    branch = jnp.einsum("bjk,bkr->bjr", right, grad_mixed, preferred_element_type=F32)
    following = (grad.astype(F32) + branch).astype(BF16)
    return following, right_term.astype(BF16), left_term.astype(BF16)


def body(inputs, cotangent, right_factor, left_factor):
    sections = lax.axis_size("s")
    groups = lax.axis_size("t")
    peers = lax.axis_size("x")
    loops, _, held, size, _ = right_factor.shape
    rows = inputs.shape[2]
    sub = held // sections
    own = sub * groups
    layers = loops * sections
    micros = sections // groups
    s_index = lax.axis_index("s")
    t_index = lax.axis_index("t")
    line = (s_index % micros) * groups + t_index
    order = group_order(size, sections, groups, peers)

    def pick(parts, index):
        return lax.dynamic_index_in_dim(parts, index, 0, keepdims=False)

    def turned(parts, send_by, place_by, target):
        moved = []
        for mask in range(sections):
            pairs = [(s * groups + t, target(s, t, mask)) for s in range(sections) for t in range(groups)]
            moved.append(lax.ppermute(pick(parts, send_by ^ mask), ("s", "t"), pairs))
        moved = jnp.stack(moved)
        return jnp.stack([pick(moved, place_by ^ part) for part in range(sections)])

    def into(s, t, mask):
        return (((s % micros) * groups + t) ^ mask) * groups + s // micros

    def outof(s, t, mask):
        line_to = s ^ mask
        return (t * micros + line_to // groups) * groups + line_to % groups

    def arriving(acts):
        parts = turned(acts.reshape(sections, sub, size, rows), line, s_index, into)
        parts = parts.reshape(micros, own, size, rows).transpose(1, 2, 0, 3)
        return parts.reshape(own, size, micros * rows)

    def settled(parts):
        return jnp.einsum("aj,bjr->bar", order, parts, preferred_element_type=F32).astype(BF16)

    def unsettled(acts):
        return jnp.einsum("aj,bar->bjr", order, acts, preferred_element_type=F32).astype(BF16)

    def leave(acts):
        parts = acts.reshape(own, size, micros, rows).transpose(2, 0, 1, 3)
        parts = turned(parts.reshape(sections, sub, size, rows), s_index, line, outof)
        return parts.reshape(1, held * size, rows)

    def scattered(*kinds):
        moved = [jnp.stack([pick(parts, s_index) for parts in kinds])]
        for mask in range(1, sections):
            pairs = [(s, s ^ mask) for s in range(sections)]
            value = jnp.stack([pick(parts, s_index ^ mask) for parts in kinds])
            moved.append(lax.ppermute(value, "s", pairs))
        moved = jnp.stack(moved)
        return [pick(moved, s_index ^ section) for section in range(sections)]

    def ordered(part):
        return jnp.einsum("aj,fbjk,ck->fbac", order, part, order, preferred_element_type=F32).astype(BF16)

    def gathered(part):
        return lax.all_gather(part, "t", axis=0, tiled=False)

    def around(value_of):
        moved = [value_of(0)]
        for mask in range(1, groups):
            moved.append(lax.ppermute(value_of(mask), "t", [(t, t ^ mask) for t in range(groups)]))
        return moved

    def gathered_directly(part):
        moved = jnp.stack(around(lambda mask: part))
        return jnp.stack([pick(moved, t_index ^ group) for group in range(groups)])

    def unordered(total):
        return jnp.einsum("aj,fbac,ck->fbjk", order, total, order, preferred_element_type=F32).astype(BF16)

    def summed(terms):
        total = lax.psum_scatter(terms.reshape(-1, size, size), "t", scatter_dimension=0, tiled=True)
        return unordered(total.reshape(terms.shape[1:]))

    def laid_out(*terms):
        return jnp.stack([term.reshape(groups, sub, size, size) for term in terms], axis=1)

    rights = right_factor[:, 0].reshape(loops, sections, sub, size, size)
    lefts = left_factor[:, 0].reshape(loops, sections, sub, size, size)
    parts = [ordered(part) for part in scattered(rights[0], lefts[0])]
    current = arriving(inputs)
    current, parts[0] = lax.optimization_barrier((current, parts[0]))
    once = 1 + s_index // sections
    first = jnp.stack([gathered_directly(parts[0][f]) for f in range(2)], axis=1)[:, None]
    starts = [0, 1] + list(range(PAIRED, layers, PAIRED)) + [layers]
    first, parts[1] = lax.optimization_barrier((first, parts[1]))
    ahead = gathered(jnp.stack(parts[1:2]))
    weights = {}
    stored = {}
    current = settled(current)

    def factors_of(layer):
        full, step = weights[layer]
        return [full[:, step, f].reshape(own, size, size) for f in range(2)]

    def forward_stretch(stretch):
        def run(_, carry):
            acts = carry[0]
            saved = []
            for layer in stretch:
                acts, pair = forward_layer(acts, *factors_of(layer))
                saved += pair
            return (acts, *saved[1:])

        return run

    for begin, end in zip(starts, starts[1:]):
        stretch = range(begin, end)
        full = ahead if begin else first
        if begin:
            coming = range(end, min(end + PAIRED, layers))
            if begin == PAIRED:
                current, rights, lefts = lax.optimization_barrier((current, rights[1:], lefts[1:]))
                for loop in range(loops - 1):
                    parts.extend(ordered(part) for part in scattered(rights[loop], lefts[loop]))
            if coming:
                ahead = gathered(jnp.stack([parts[layer] for layer in coming]))
        weights.update((layer, (full, layer - begin)) for layer in stretch)
        blanks = [jnp.zeros(current.shape, BF16) for _ in range(2 * len(stretch) - 1)]
        entered = current
        current, *saved = lax.fori_loop(0, once, forward_stretch(stretch), (current, *blanks))
        current, ahead = lax.optimization_barrier((current, ahead))
        saved = [entered] + saved
        stored.update((layer, saved[2 * step : 2 * step + 2]) for step, layer in enumerate(stretch))
    current, cotangent = lax.optimization_barrier((current, cotangent))
    grad = settled(arriving(cotangent))
    outputs = leave(unsettled(current))

    sums = [None] * layers

    def backward_pair(top):
        def run(_, carry):
            grad, _ = carry
            terms = []
            for layer in range(top, top - PAIRED, -1):
                grad, *pair = backward_layer(grad, *factors_of(layer), stored[layer])
                terms += pair
            return grad, laid_out(*terms)

        return run

    totals = {}
    for top in range(layers - 1, 0, -PAIRED):
        blank = jnp.zeros((groups, 2 * PAIRED, sub, size, size), BF16)
        grad, terms = lax.fori_loop(0, once, backward_pair(top), (grad, blank))
        if top + 2 * PAIRED in totals:
            asked = totals[top + 2 * PAIRED]
            grad, terms, totals[top + 2 * PAIRED] = lax.optimization_barrier((grad, terms, asked))
        totals[top] = summed(terms)
    grad = lax.fori_loop(0, once, lambda _, acts: unsettled(acts), grad)
    if 2 * PAIRED <= layers:
        grad, totals[2 * PAIRED - 1] = lax.optimization_barrier((grad, totals[2 * PAIRED - 1]))
    for top, total in totals.items():
        for step in range(PAIRED):
            sums[top - step] = [total[2 * step], total[2 * step + 1]]
    input_grad = leave(grad)

    def of_loop(loop, factor):
        return jnp.stack([sums[loop * sections + section][factor] for section in range(sections)])

    halves = []
    for loop in range(loops):
        moved = jnp.stack(scattered(of_loop(loop, 0), of_loop(loop, 1)), axis=1)
        halves.append(moved.reshape(2, 1, held, size, size))
    grads = jnp.stack(halves).astype(F32)
    return (outputs, input_grad, grads[:, 0], grads[:, 1])


def solution(mesh):
    sections = mesh.shape["section"]
    peers = mesh.shape["block"] // GROUPS
    grouped = Mesh(mesh.devices.reshape(sections, GROUPS, peers), ("s", "t", "x"))
    acts = P("s", ("t", "x"), None)
    factor = P(None, "s", ("t", "x"), None, None)
    return jax.shard_map(
        body,
        mesh=grouped,
        in_specs=(acts, acts, factor, factor),
        out_specs=(acts, acts, factor, factor),
        check_vma=False,
    )
```

```python
import jax
import jax.numpy as jnp
from jax import lax
from jax.sharding import Mesh, PartitionSpec as P

F32 = jnp.float32
BF16 = jnp.bfloat16
WIDE = ("s", "x")
GROUPS = 4
PAIRED = 2


def silu_slope(values):
    sigmoid = jax.nn.sigmoid(values)
    return sigmoid * (1.0 + values * (1.0 - sigmoid))


def group_order(size, sections, groups, peers):
    natural = jnp.arange(size).reshape(groups, peers, sections, -1)
    order = natural.transpose(2, 1, 0, 3).reshape(size)
    return (order[:, None] == jnp.arange(size)[None, :]).astype(BF16)


def exchange(values):
    own, full, rows = values.shape
    pieces = values.transpose(1, 0, 2).reshape(full // own, own, own, rows)
    moved = lax.all_to_all(pieces, WIDE, split_axis=0, concat_axis=0, tiled=True)
    return moved.transpose(1, 0, 2, 3).reshape(own, full, rows)


def forward_layer(acts, right, left):
    mixed = jnp.einsum("bjk,bjr->bkr", right, acts, preferred_element_type=F32).astype(BF16)
    columns = exchange(mixed)
    activated = jax.nn.silu(columns.astype(F32)).astype(BF16)
    second = jnp.einsum("kbc,kbr->kcr", left, activated, preferred_element_type=F32).astype(BF16)
    following = (acts.astype(F32) + exchange(second).astype(F32)).astype(BF16)
    return following, (acts, columns)


def backward_layer(grad, right, left, saved):
    acts, columns = saved
    grad_columns = exchange(grad)
    wide = columns.astype(F32)
    activated = jax.nn.silu(wide).astype(BF16)
    left_term = jnp.einsum("kbr,kcr->kbc", activated, grad_columns, preferred_element_type=F32)
    grad_act = jnp.einsum("kbc,kcr->kbr", left, grad_columns, preferred_element_type=F32)
    grad_mixed = exchange((grad_act * silu_slope(wide)).astype(BF16))
    right_term = jnp.einsum("bjr,bkr->bjk", acts, grad_mixed, preferred_element_type=F32)
    branch = jnp.einsum("bjk,bkr->bjr", right, grad_mixed, preferred_element_type=F32)
    following = (grad.astype(F32) + branch).astype(BF16)
    return following, right_term.astype(BF16), left_term.astype(BF16)


def body(inputs, cotangent, right_factor, left_factor):
    sections = lax.axis_size("s")
    groups = lax.axis_size("t")
    peers = lax.axis_size("x")
    loops, _, held, size, _ = right_factor.shape
    rows = inputs.shape[2]
    sub = held // sections
    own = sub * groups
    layers = loops * sections
    micros = sections // groups
    s_index = lax.axis_index("s")
    t_index = lax.axis_index("t")
    line = (s_index % micros) * groups + t_index
    order = group_order(size, sections, groups, peers)

    def pick(parts, index):
        return lax.dynamic_index_in_dim(parts, index, 0, keepdims=False)

    def sent(parts, send_by, target):
        moved = []
        for mask in range(sections):
            pairs = [(s * groups + t, target(s, t, mask)) for s in range(sections) for t in range(groups)]
            moved.append(lax.ppermute(pick(parts, send_by ^ mask), ("s", "t"), pairs))
        return moved

    def placed(moved, place_by):
        moved = jnp.stack(moved)
        return jnp.stack([pick(moved, place_by ^ part) for part in range(sections)])

    def into(s, t, mask):
        return (((s % micros) * groups + t) ^ mask) * groups + s // micros

    def outof(s, t, mask):
        line_to = s ^ mask
        return (t * micros + line_to // groups) * groups + line_to % groups

    def arriving(acts):
        return sent(acts.reshape(sections, sub, size, rows), line, into)

    def arrived(moved):
        parts = placed(moved, s_index).reshape(micros, own, size, rows).transpose(1, 2, 0, 3)
        return parts.reshape(own, size, micros * rows)

    def settled(parts):
        return jnp.einsum("aj,bjr->bar", order, parts, preferred_element_type=F32).astype(BF16)

    def unsettled(acts):
        return jnp.einsum("aj,bar->bjr", order, acts, preferred_element_type=F32).astype(BF16)

    def leave(acts):
        parts = acts.reshape(own, size, micros, rows).transpose(2, 0, 1, 3)
        parts = placed(sent(parts.reshape(sections, sub, size, rows), s_index, outof), line)
        return parts.reshape(1, held * size, rows)

    def scattered(*kinds):
        moved = [jnp.stack([pick(parts, s_index) for parts in kinds])]
        for mask in range(1, sections):
            pairs = [(s, s ^ mask) for s in range(sections)]
            value = jnp.stack([pick(parts, s_index ^ mask) for parts in kinds])
            moved.append(lax.ppermute(value, "s", pairs))
        moved = jnp.stack(moved)
        return [pick(moved, s_index ^ section) for section in range(sections)]

    def ordered(part):
        return jnp.einsum("aj,fbjk,ck->fbac", order, part, order, preferred_element_type=F32).astype(BF16)

    def gathered(part):
        return lax.all_gather(part, "t", axis=0, tiled=False)

    def around(value_of):
        moved = [value_of(0)]
        for mask in range(1, groups):
            moved.append(lax.ppermute(value_of(mask), "t", [(t, t ^ mask) for t in range(groups)]))
        return moved

    def gathered_directly(part):
        moved = jnp.stack(around(lambda mask: part))
        return jnp.stack([pick(moved, t_index ^ group) for group in range(groups)])

    def unordered(total):
        return jnp.einsum("aj,fbac,ck->fbjk", order, total, order, preferred_element_type=F32).astype(BF16)

    def summed(terms):
        total = lax.psum_scatter(terms.reshape(-1, size, size), "t", scatter_dimension=0, tiled=True)
        return unordered(total.reshape(terms.shape[1:]))

    def laid_out(*terms):
        return jnp.stack([term.reshape(groups, sub, size, size) for term in terms], axis=1)

    rights = right_factor[:, 0].reshape(loops, sections, sub, size, size)
    lefts = left_factor[:, 0].reshape(loops, sections, sub, size, size)
    parts = [ordered(part) for part in scattered(rights[0], lefts[0])]
    current = arrived(arriving(inputs))
    current, parts[0] = lax.optimization_barrier((current, parts[0]))
    once = 1 + s_index // sections
    first = jnp.stack([gathered_directly(parts[0][f]) for f in range(2)], axis=1)[:, None]
    starts = [0, 1] + list(range(PAIRED, layers, PAIRED)) + [layers]
    first, parts[1] = lax.optimization_barrier((first, parts[1]))
    ahead = gathered(jnp.stack(parts[1:2]))
    weights = {}
    stored = {}
    current = settled(current)

    def factors_of(layer):
        full, step = weights[layer]
        return [full[:, step, f].reshape(own, size, size) for f in range(2)]

    def forward_stretch(stretch):
        def run(_, carry):
            acts = carry[0]
            saved = []
            for layer in stretch:
                acts, pair = forward_layer(acts, *factors_of(layer))
                saved += pair
            return (acts, *saved[1:])

        return run

    for begin, end in zip(starts, starts[1:]):
        stretch = range(begin, end)
        full = first
        if begin:
            coming = range(end, min(end + PAIRED, layers))
            if begin == PAIRED:
                current, rights, lefts = lax.optimization_barrier((current, rights[1:], lefts[1:]))
                for loop in range(loops - 1):
                    parts.extend(ordered(part) for part in scattered(rights[loop], lefts[loop]))
                ahead, parts[end:] = lax.optimization_barrier((ahead, parts[end:]))
            full = ahead
            if coming:
                ahead = gathered(jnp.stack([parts[layer] for layer in coming]))
        if end == layers:
            current, cotangent = lax.optimization_barrier((current, cotangent))
            moving = arriving(cotangent)
        weights.update((layer, (full, layer - begin)) for layer in stretch)
        blanks = [jnp.zeros(current.shape, BF16) for _ in range(2 * len(stretch) - 1)]
        entered = current
        current, *saved = lax.fori_loop(0, once, forward_stretch(stretch), (current, *blanks))
        current, ahead = lax.optimization_barrier((current, ahead))
        saved = [entered] + saved
        stored.update((layer, saved[2 * step : 2 * step + 2]) for step, layer in enumerate(stretch))
    current, moving = lax.optimization_barrier((current, moving))
    grad = settled(arrived(moving))
    outputs = leave(unsettled(current))

    sums = [None] * layers

    def backward_pair(top):
        def run(_, carry):
            grad, _ = carry
            terms = []
            for layer in range(top, top - PAIRED, -1):
                grad, *pair = backward_layer(grad, *factors_of(layer), stored[layer])
                terms += pair
            return grad, laid_out(*terms)

        return run

    totals = {}
    for top in range(layers - 1, 0, -PAIRED):
        blank = jnp.zeros((groups, 2 * PAIRED, sub, size, size), BF16)
        grad, terms = lax.fori_loop(0, once, backward_pair(top), (grad, blank))
        if top + 2 * PAIRED in totals:
            asked = totals[top + 2 * PAIRED]
            grad, terms, totals[top + 2 * PAIRED] = lax.optimization_barrier((grad, terms, asked))
        totals[top] = summed(terms)
    grad = lax.fori_loop(0, once, lambda _, acts: unsettled(acts), grad)
    if 2 * PAIRED <= layers:
        _, totals[2 * PAIRED - 1] = lax.optimization_barrier((grad, totals[2 * PAIRED - 1]))
    for top, total in totals.items():
        for step in range(PAIRED):
            sums[top - step] = [total[2 * step], total[2 * step + 1]]
    input_grad = leave(grad)

    def of_loop(loop, factor):
        return jnp.stack([sums[loop * sections + section][factor] for section in range(sections)])

    halves = []
    for loop in range(loops):
        moved = jnp.stack(scattered(of_loop(loop, 0), of_loop(loop, 1)), axis=1)
        halves.append(moved.reshape(2, 1, held, size, size))
    grads = jnp.stack(halves).astype(F32)
    return (outputs, input_grad, grads[:, 0], grads[:, 1])


def solution(mesh):
    sections = mesh.shape["section"]
    peers = mesh.shape["block"] // GROUPS
    grouped = Mesh(mesh.devices.reshape(sections, GROUPS, peers), ("s", "t", "x"))
    acts = P("s", ("t", "x"), None)
    factor = P(None, "s", ("t", "x"), None, None)
    return jax.shard_map(
        body,
        mesh=grouped,
        in_specs=(acts, acts, factor, factor),
        out_specs=(acts, acts, factor, factor),
        check_vma=False,
    )
```

```python
import jax
import jax.numpy as jnp
from jax import lax
from jax.sharding import Mesh, PartitionSpec as P

F32 = jnp.float32
BF16 = jnp.bfloat16
WIDE = ("s", "x")
GROUPS = 4
PAIRED = 2


def silu_slope(values):
    sigmoid = jax.nn.sigmoid(values)
    return sigmoid * (1.0 + values * (1.0 - sigmoid))


def group_order(size, sections, groups, peers):
    natural = jnp.arange(size).reshape(groups, peers, sections, -1)
    order = natural.transpose(2, 1, 0, 3).reshape(size)
    return (order[:, None] == jnp.arange(size)[None, :]).astype(BF16)


def exchange(values):
    own, full, rows = values.shape
    pieces = values.transpose(1, 0, 2).reshape(full // own, own, own, rows)
    moved = lax.all_to_all(pieces, WIDE, split_axis=0, concat_axis=0, tiled=True)
    return moved.transpose(1, 0, 2, 3).reshape(own, full, rows)


def forward_layer(acts, right, left):
    mixed = jnp.einsum("bjk,bjr->bkr", right, acts, preferred_element_type=F32).astype(BF16)
    columns = exchange(mixed)
    activated = jax.nn.silu(columns.astype(F32)).astype(BF16)
    second = jnp.einsum("kbc,kbr->kcr", left, activated, preferred_element_type=F32).astype(BF16)
    following = (acts.astype(F32) + exchange(second).astype(F32)).astype(BF16)
    return following, (acts, columns)


def backward_layer(grad, right, left, saved):
    acts, columns = saved
    grad_columns = exchange(grad)
    wide = columns.astype(F32)
    activated = jax.nn.silu(wide).astype(BF16)
    left_term = jnp.einsum("kbr,kcr->kbc", activated, grad_columns, preferred_element_type=F32)
    grad_act = jnp.einsum("kbc,kcr->kbr", left, grad_columns, preferred_element_type=F32)
    grad_mixed = exchange((grad_act * silu_slope(wide)).astype(BF16))
    right_term = jnp.einsum("bjr,bkr->bjk", acts, grad_mixed, preferred_element_type=F32)
    branch = jnp.einsum("bjk,bkr->bjr", right, grad_mixed, preferred_element_type=F32)
    following = (grad.astype(F32) + branch).astype(BF16)
    return following, right_term.astype(BF16), left_term.astype(BF16)


def body(inputs, cotangent, right_factor, left_factor):
    sections = lax.axis_size("s")
    groups = lax.axis_size("t")
    peers = lax.axis_size("x")
    loops, _, held, size, _ = right_factor.shape
    rows = inputs.shape[2]
    sub = held // sections
    own = sub * groups
    layers = loops * sections
    micros = sections // groups
    s_index = lax.axis_index("s")
    t_index = lax.axis_index("t")
    line = (s_index % micros) * groups + t_index
    order = group_order(size, sections, groups, peers)

    def pick(parts, index):
        return lax.dynamic_index_in_dim(parts, index, 0, keepdims=False)

    def turned(parts, send_by, place_by, target):
        moved = []
        for mask in range(sections):
            pairs = [(s * groups + t, target(s, t, mask)) for s in range(sections) for t in range(groups)]
            moved.append(lax.ppermute(pick(parts, send_by ^ mask), ("s", "t"), pairs))
        moved = jnp.stack(moved)
        return jnp.stack([pick(moved, place_by ^ part) for part in range(sections)])

    def into(s, t, mask):
        return (((s % micros) * groups + t) ^ mask) * groups + s // micros

    def outof(s, t, mask):
        line_to = s ^ mask
        return (t * micros + line_to // groups) * groups + line_to % groups

    def arriving(acts):
        parts = turned(acts.reshape(sections, sub, size, rows), line, s_index, into)
        parts = parts.reshape(micros, own, size, rows).transpose(1, 2, 0, 3)
        return parts.reshape(own, size, micros * rows)

    def settled(parts):
        return jnp.einsum("aj,bjr->bar", order, parts, preferred_element_type=F32).astype(BF16)

    def unsettled(acts):
        return jnp.einsum("aj,bar->bjr", order, acts, preferred_element_type=F32).astype(BF16)

    def leave(acts):
        parts = acts.reshape(own, size, micros, rows).transpose(2, 0, 1, 3)
        parts = turned(parts.reshape(sections, sub, size, rows), s_index, line, outof)
        return parts.reshape(1, held * size, rows)

    def dealt(*kinds):
        moved = [jnp.stack([pick(parts, s_index) for parts in kinds])]
        for mask in range(1, sections):
            pairs = [(s, s ^ mask) for s in range(sections)]
            value = jnp.stack([pick(parts, s_index ^ mask) for parts in kinds])
            moved.append(lax.ppermute(value, "s", pairs))
        return moved

    def collected(moved):
        moved = jnp.stack(moved)
        return [pick(moved, s_index ^ section) for section in range(sections)]

    def scattered(*kinds):
        return collected(dealt(*kinds))

    def ordered(part):
        return jnp.einsum("aj,fbjk,ck->fbac", order, part, order, preferred_element_type=F32).astype(BF16)

    def gathered(part):
        return lax.all_gather(part, "t", axis=0, tiled=False)

    def around(value_of):
        moved = [value_of(0)]
        for mask in range(1, groups):
            moved.append(lax.ppermute(value_of(mask), "t", [(t, t ^ mask) for t in range(groups)]))
        return moved

    def gathered_directly(part):
        moved = jnp.stack(around(lambda mask: part))
        return jnp.stack([pick(moved, t_index ^ group) for group in range(groups)])

    def unordered(total):
        return jnp.einsum("aj,fbac,ck->fbjk", order, total, order, preferred_element_type=F32).astype(BF16)

    def summed(terms):
        total = lax.psum_scatter(terms.reshape(-1, size, size), "t", scatter_dimension=0, tiled=True)
        return unordered(total.reshape(terms.shape[1:]))

    def laid_out(*terms):
        return jnp.stack([term.reshape(groups, sub, size, size) for term in terms], axis=1)

    rights = right_factor[:, 0].reshape(loops, sections, sub, size, size)
    lefts = left_factor[:, 0].reshape(loops, sections, sub, size, size)
    parts = [ordered(part) for part in scattered(rights[0], lefts[0])]
    current = arriving(inputs)
    current, parts[0] = lax.optimization_barrier((current, parts[0]))
    once = 1 + s_index // sections
    first = jnp.stack([gathered_directly(parts[0][f]) for f in range(2)], axis=1)[:, None]
    starts = [0, 1] + list(range(PAIRED, layers, PAIRED)) + [layers]
    first, parts[1] = lax.optimization_barrier((first, parts[1]))
    ahead = gathered(jnp.stack(parts[1:2]))
    weights = {}
    stored = {}
    current = settled(current)

    def factors_of(layer):
        full, step = weights[layer]
        return [full[:, step, f].reshape(own, size, size) for f in range(2)]

    def forward_stretch(stretch):
        def run(_, carry):
            acts = carry[0]
            saved = []
            for layer in stretch:
                acts, pair = forward_layer(acts, *factors_of(layer))
                saved += pair
            return (acts, *saved[1:])

        return run

    for begin, end in zip(starts, starts[1:]):
        stretch = range(begin, end)
        full = ahead if begin else first
        if begin:
            coming = range(end, min(end + PAIRED, layers))
            if begin == 1:
                current, rights, lefts = lax.optimization_barrier((current, rights[1:], lefts[1:]))
                moving = [dealt(rights[loop], lefts[loop]) for loop in range(loops - 1)]
            if coming:
                ahead = gathered(jnp.stack([parts[layer] for layer in coming]))
        weights.update((layer, (full, layer - begin)) for layer in stretch)
        blanks = [jnp.zeros(current.shape, BF16) for _ in range(2 * len(stretch) - 1)]
        entered = current
        current, *saved = lax.fori_loop(0, once, forward_stretch(stretch), (current, *blanks))
        current, ahead = lax.optimization_barrier((current, ahead))
        if begin == 1:
            current, moving = lax.optimization_barrier((current, moving))
            parts.extend(ordered(part) for moved in moving for part in collected(moved))
        saved = [entered] + saved
        stored.update((layer, saved[2 * step : 2 * step + 2]) for step, layer in enumerate(stretch))
    current, cotangent = lax.optimization_barrier((current, cotangent))
    grad = settled(arriving(cotangent))
    outputs = leave(unsettled(current))

    sums = [None] * layers

    def backward_pair(top):
        def run(_, carry):
            grad, _ = carry
            terms = []
            for layer in range(top, top - PAIRED, -1):
                grad, *pair = backward_layer(grad, *factors_of(layer), stored[layer])
                terms += pair
            return grad, laid_out(*terms)

        return run

    totals = {}
    for top in range(layers - 1, 0, -PAIRED):
        blank = jnp.zeros((groups, 2 * PAIRED, sub, size, size), BF16)
        grad, terms = lax.fori_loop(0, once, backward_pair(top), (grad, blank))
        if top + 2 * PAIRED in totals:
            asked = totals[top + 2 * PAIRED]
            grad, terms, totals[top + 2 * PAIRED] = lax.optimization_barrier((grad, terms, asked))
        totals[top] = summed(terms)
    grad = lax.fori_loop(0, once, lambda _, acts: unsettled(acts), grad)
    if 2 * PAIRED <= layers:
        grad, totals[2 * PAIRED - 1] = lax.optimization_barrier((grad, totals[2 * PAIRED - 1]))
    for top, total in totals.items():
        for step in range(PAIRED):
            sums[top - step] = [total[2 * step], total[2 * step + 1]]
    input_grad = leave(grad)

    def of_loop(loop, factor):
        return jnp.stack([sums[loop * sections + section][factor] for section in range(sections)])

    halves = []
    for loop in range(loops):
        moved = jnp.stack(scattered(of_loop(loop, 0), of_loop(loop, 1)), axis=1)
        halves.append(moved.reshape(2, 1, held, size, size))
    grads = jnp.stack(halves).astype(F32)
    return (outputs, input_grad, grads[:, 0], grads[:, 1])


def solution(mesh):
    sections = mesh.shape["section"]
    peers = mesh.shape["block"] // GROUPS
    grouped = Mesh(mesh.devices.reshape(sections, GROUPS, peers), ("s", "t", "x"))
    acts = P("s", ("t", "x"), None)
    factor = P(None, "s", ("t", "x"), None, None)
    return jax.shard_map(
        body,
        mesh=grouped,
        in_specs=(acts, acts, factor, factor),
        out_specs=(acts, acts, factor, factor),
        check_vma=False,
    )
```

```python
import jax
import jax.numpy as jnp
from jax import lax
from jax.sharding import Mesh, PartitionSpec as P

F32 = jnp.float32
BF16 = jnp.bfloat16
WIDE = ("s", "x")
GROUPS = 4
PAIRED = 2


def silu_slope(values):
    sigmoid = jax.nn.sigmoid(values)
    return sigmoid * (1.0 + values * (1.0 - sigmoid))


def group_order(size, sections, groups, peers):
    natural = jnp.arange(size).reshape(groups, peers, sections, -1)
    order = natural.transpose(2, 1, 0, 3).reshape(size)
    return (order[:, None] == jnp.arange(size)[None, :]).astype(BF16)


def exchange(values):
    own, full, rows = values.shape
    pieces = values.transpose(1, 0, 2).reshape(full // own, own, own, rows)
    moved = lax.all_to_all(pieces, WIDE, split_axis=0, concat_axis=0, tiled=True)
    return moved.transpose(1, 0, 2, 3).reshape(own, full, rows)


def forward_layer(acts, right, left):
    mixed = jnp.einsum("bjk,bjr->bkr", right, acts, preferred_element_type=F32).astype(BF16)
    columns = exchange(mixed)
    activated = jax.nn.silu(columns.astype(F32)).astype(BF16)
    second = jnp.einsum("kbc,kbr->kcr", left, activated, preferred_element_type=F32).astype(BF16)
    following = (acts.astype(F32) + exchange(second).astype(F32)).astype(BF16)
    return following, (acts, columns)


def backward_layer(grad, right, left, saved):
    acts, columns = saved
    grad_columns = exchange(grad)
    wide = columns.astype(F32)
    activated = jax.nn.silu(wide).astype(BF16)
    left_term = jnp.einsum("kbr,kcr->kbc", activated, grad_columns, preferred_element_type=F32)
    grad_act = jnp.einsum("kbc,kcr->kbr", left, grad_columns, preferred_element_type=F32)
    grad_mixed = exchange((grad_act * silu_slope(wide)).astype(BF16))
    right_term = jnp.einsum("bjr,bkr->bjk", acts, grad_mixed, preferred_element_type=F32)
    branch = jnp.einsum("bjk,bkr->bjr", right, grad_mixed, preferred_element_type=F32)
    following = (grad.astype(F32) + branch).astype(BF16)
    return following, right_term.astype(BF16), left_term.astype(BF16)


def body(inputs, cotangent, right_factor, left_factor):
    sections = lax.axis_size("s")
    groups = lax.axis_size("t")
    peers = lax.axis_size("x")
    loops, _, held, size, _ = right_factor.shape
    rows = inputs.shape[2]
    sub = held // sections
    own = sub * groups
    layers = loops * sections
    micros = sections // groups
    s_index = lax.axis_index("s")
    t_index = lax.axis_index("t")
    line = (s_index % micros) * groups + t_index
    order = group_order(size, sections, groups, peers)

    def pick(parts, index):
        return lax.dynamic_index_in_dim(parts, index, 0, keepdims=False)

    def turned(parts, send_by, place_by, target):
        moved = []
        for mask in range(sections):
            pairs = [(s * groups + t, target(s, t, mask)) for s in range(sections) for t in range(groups)]
            moved.append(lax.ppermute(pick(parts, send_by ^ mask), ("s", "t"), pairs))
        moved = jnp.stack(moved)
        return jnp.stack([pick(moved, place_by ^ part) for part in range(sections)])

    def into(s, t, mask):
        return (((s % micros) * groups + t) ^ mask) * groups + s // micros

    def outof(s, t, mask):
        line_to = s ^ mask
        return (t * micros + line_to // groups) * groups + line_to % groups

    def arriving(acts):
        parts = turned(acts.reshape(sections, sub, size, rows), line, s_index, into)
        parts = parts.reshape(micros, own, size, rows).transpose(1, 2, 0, 3)
        return parts.reshape(own, size, micros * rows)

    def settled(parts):
        return jnp.einsum("aj,bjr->bar", order, parts, preferred_element_type=F32).astype(BF16)

    def unsettled(acts):
        return jnp.einsum("aj,bar->bjr", order, acts, preferred_element_type=F32).astype(BF16)

    def leave(acts):
        parts = acts.reshape(own, size, micros, rows).transpose(2, 0, 1, 3)
        parts = turned(parts.reshape(sections, sub, size, rows), s_index, line, outof)
        return parts.reshape(1, held * size, rows)

    def dealt(*kinds):
        moved = [jnp.stack([pick(parts, s_index) for parts in kinds])]
        for mask in range(1, sections):
            pairs = [(s, s ^ mask) for s in range(sections)]
            value = jnp.stack([pick(parts, s_index ^ mask) for parts in kinds])
            moved.append(lax.ppermute(value, "s", pairs))
        return moved

    def collected(moved):
        moved = jnp.stack(moved)
        return [pick(moved, s_index ^ section) for section in range(sections)]

    def scattered(*kinds):
        return collected(dealt(*kinds))

    def ordered(part):
        return jnp.einsum("aj,fbjk,ck->fbac", order, part, order, preferred_element_type=F32).astype(BF16)

    def gathered(part):
        return lax.all_gather(part, "t", axis=0, tiled=False)

    def around(value_of):
        moved = [value_of(0)]
        for mask in range(1, groups):
            moved.append(lax.ppermute(value_of(mask), "t", [(t, t ^ mask) for t in range(groups)]))
        return moved

    def gathered_directly(part):
        moved = jnp.stack(around(lambda mask: part))
        return jnp.stack([pick(moved, t_index ^ group) for group in range(groups)])

    def unordered(total):
        return jnp.einsum("aj,fbac,ck->fbjk", order, total, order, preferred_element_type=F32).astype(BF16)

    def summed(terms):
        total = lax.psum_scatter(terms.reshape(-1, size, size), "t", scatter_dimension=0, tiled=True)
        return unordered(total.reshape(terms.shape[1:]))

    def laid_out(*terms):
        return jnp.stack([term.reshape(groups, sub, size, size) for term in terms], axis=1)

    rights = right_factor[:, 0].reshape(loops, sections, sub, size, size)
    lefts = left_factor[:, 0].reshape(loops, sections, sub, size, size)
    moving = dealt(rights[0], lefts[0])
    moving[0], inputs = lax.optimization_barrier((moving[0], inputs))
    parts = [ordered(part) for part in collected(moving)]
    current = arriving(inputs)
    once = 1 + s_index // sections
    first = jnp.stack([gathered_directly(parts[0][f]) for f in range(2)], axis=1)[:, None]
    starts = [0, 1] + list(range(PAIRED, layers, PAIRED)) + [layers]
    first, parts[1] = lax.optimization_barrier((first, parts[1]))
    ahead = gathered(jnp.stack(parts[1:2]))
    weights = {}
    stored = {}
    current = settled(current)

    def factors_of(layer):
        full, step = weights[layer]
        return [full[:, step, f].reshape(own, size, size) for f in range(2)]

    def forward_stretch(stretch):
        def run(_, carry):
            acts = carry[0]
            saved = []
            for layer in stretch:
                acts, pair = forward_layer(acts, *factors_of(layer))
                saved += pair
            return (acts, *saved[1:])

        return run

    for begin, end in zip(starts, starts[1:]):
        stretch = range(begin, end)
        full = ahead if begin else first
        if begin:
            coming = range(end, min(end + PAIRED, layers))
            if begin == 1:
                current, rights, lefts = lax.optimization_barrier((current, rights[1:], lefts[1:]))
                moving = [dealt(rights[loop], lefts[loop]) for loop in range(loops - 1)]
            if coming:
                ahead = gathered(jnp.stack([parts[layer] for layer in coming]))
        weights.update((layer, (full, layer - begin)) for layer in stretch)
        blanks = [jnp.zeros(current.shape, BF16) for _ in range(2 * len(stretch) - 1)]
        entered = current
        current, *saved = lax.fori_loop(0, once, forward_stretch(stretch), (current, *blanks))
        current, ahead = lax.optimization_barrier((current, ahead))
        if begin == 1:
            current, moving = lax.optimization_barrier((current, moving))
            parts.extend(ordered(part) for moved in moving for part in collected(moved))
        saved = [entered] + saved
        stored.update((layer, saved[2 * step : 2 * step + 2]) for step, layer in enumerate(stretch))
    current, cotangent = lax.optimization_barrier((current, cotangent))
    grad = settled(arriving(cotangent))
    outputs = leave(unsettled(current))

    sums = [None] * layers

    def backward_pair(top):
        def run(_, carry):
            grad, _ = carry
            terms = []
            for layer in range(top, top - PAIRED, -1):
                grad, *pair = backward_layer(grad, *factors_of(layer), stored[layer])
                terms += pair
            return grad, laid_out(*terms)

        return run

    totals = {}
    for top in range(layers - 1, 0, -PAIRED):
        blank = jnp.zeros((groups, 2 * PAIRED, sub, size, size), BF16)
        grad, terms = lax.fori_loop(0, once, backward_pair(top), (grad, blank))
        if top + 2 * PAIRED in totals:
            asked = totals[top + 2 * PAIRED]
            grad, terms, totals[top + 2 * PAIRED] = lax.optimization_barrier((grad, terms, asked))
        totals[top] = summed(terms)
    grad = lax.fori_loop(0, once, lambda _, acts: unsettled(acts), grad)
    if 2 * PAIRED <= layers:
        _, totals[2 * PAIRED - 1] = lax.optimization_barrier((grad, totals[2 * PAIRED - 1]))
    for top, total in totals.items():
        for step in range(PAIRED):
            sums[top - step] = [total[2 * step], total[2 * step + 1]]
    input_grad = leave(grad)

    def of_loop(loop, factor):
        return jnp.stack([sums[loop * sections + section][factor] for section in range(sections)])

    halves = []
    for loop in range(loops):
        moved = jnp.stack(scattered(of_loop(loop, 0), of_loop(loop, 1)), axis=1)
        halves.append(moved.reshape(2, 1, held, size, size))
    grads = jnp.stack(halves).astype(F32)
    return (outputs, input_grad, grads[:, 0], grads[:, 1])


def solution(mesh):
    sections = mesh.shape["section"]
    peers = mesh.shape["block"] // GROUPS
    grouped = Mesh(mesh.devices.reshape(sections, GROUPS, peers), ("s", "t", "x"))
    acts = P("s", ("t", "x"), None)
    factor = P(None, "s", ("t", "x"), None, None)
    return jax.shard_map(
        body,
        mesh=grouped,
        in_specs=(acts, acts, factor, factor),
        out_specs=(acts, acts, factor, factor),
        check_vma=False,
    )
```
